256 devices in a mesh: row: 32 (over x, y, core), col: 8 (over z).
Axes of the slice: x: 4, y: 4, z: 8, core: 2. Of those that a mesh axis runs over, the one named last changes fastest.
Arguments:
- embeddings: bfloat16 [32768, 2048], P(('row', 'col')), may hold values from -6 to 6
- inverse_scales: float32 [2048], replicated, may hold values from 0.0039774757 to 0.059662133
- matches: int32 [32768, 2], replicated, may hold values from 0 to 32767
Outputs:
- trailing: float32 [32768, 4096], P('row', 'col')
- factor: float32 [32768, 1024], P(('row', 'col'))
The draws below stay inside these ranges and needn't reach their ends.
Inputs may be any that keep to these rules, and one draw needn't show every extreme that they name: `matches`: candidate indices of the winner and the loser of each match.
All inputs are finite; a program needn't handle non-finite values.
Results may differ from the reference program's by a relative error of at most 0.0065.
Values may be sent and summed in bfloat16 or wider, within the bound.
A program may use at most 128 MiB of HBM per device.

```python
import math
import jax
import jax.numpy as jnp
from jax import lax

R_DEV = 1024
EMBED = 2048
PANEL = 1024
STOPS = 4
CANDIDATES = 32768
MATCHES = 32768
SLICE = 128
PANEL_SHARE = 32
N_ROW = 32
N_COL = 8


def plant(array, stream_key, least, largest):
    place = [jax.random.randint(jax.random.fold_in(stream_key, axis), (), 0, length) for axis, length in enumerate(array.shape)]
    longest = array.shape.index(max(array.shape))
    neighbour = place[:longest] + [(place[longest] + 1) % array.shape[longest]] + place[longest + 1:]
    return array.at[tuple(place)].set(least).at[tuple(neighbour)].set(largest)


def levels(own_key, dims, cuts, low, top_value):
    level = 1.0
    for dim, shards_of in cuts:
        heights = jax.random.uniform(jax.random.fold_in(jax.random.fold_in(own_key, 6), dim), (shards_of,), jnp.float32, low / len(cuts), top_value / len(cuts))
        level = level * jnp.repeat(jnp.exp(heights), dims[dim] // shards_of).reshape((-1,) + (1,) * (len(dims) - 1 - dim))
    return level


def bell_draw(own_key, shape, scale, bound, split=(), held_as=jnp.bfloat16):
    entries = jax.random.normal(own_key, shape, jnp.float32) * scale
    if len(split) > 0:
        entries = levels(own_key, shape, split, -0.22, 0.18) * entries
    return jnp.clip(entries, min=-bound, max=bound).astype(held_as)


def setup_inputs(seed: int = 0) -> dict:
    keys = jax.random.split(jax.random.key(seed), 4)
    return {
        "embeddings": bell_draw(keys[0], (CANDIDATES, EMBED), 1.0, 6.0, ((0, 256),)),
        "inverse_scales": jnp.clip(jnp.exp(jax.random.uniform(keys[1], (EMBED,), jnp.float32, math.log(0.0039774757), math.log(0.059662133))), 0.0039774757, 0.059662133),
        "matches": plant(jax.random.randint(keys[2], (MATCHES, 2), 0, CANDIDATES), jax.random.fold_in(keys[2], 1), 0, CANDIDATES - 1).astype(jnp.int32),
    }


def squares_of(scaled):
    values = scaled.astype(jnp.float32)
    return jnp.sum(values * values, axis=1)

def kernel_block(left, left_sq, right, right_sq):
    inner = jnp.dot(left.astype(jnp.float32), right.T.astype(jnp.float32), preferred_element_type=jnp.float32)
    return jnp.exp(-0.5 * (left_sq[:, None] + right_sq[None, :] - 2.0 * inner))

def match_counts(identity, matches):
    total = matches.shape[0]
    group_rows = math.gcd(total, 1024)
    grouped = matches.reshape(total // group_rows, group_rows, 2)

    def accumulate(carry, group):
        hits = (group[:, 0:1] == identity[None, :]).astype(jnp.float32)
        hits = hits + (group[:, 1:2] == identity[None, :]).astype(jnp.float32)
        return (carry + jnp.sum(hits, axis=0), None)
    counts, unused = lax.scan(accumulate, jnp.zeros(identity.shape, jnp.float32), grouped)
    return 0.1 + 0.5 * counts

def reference(embeddings, inverse_scales, matches):
    scaled = (embeddings.astype(jnp.float32) * inverse_scales[None, :]).astype(jnp.bfloat16)
    squares = squares_of(scaled)
    extras = match_counts(jnp.arange(CANDIDATES, dtype=jnp.int32), matches)
    panel_ids = (jnp.arange(N_ROW, dtype=jnp.int32)[:, None] * R_DEV + jnp.arange(PANEL_SHARE, dtype=jnp.int32)[None, :]).reshape(-1)
    panel_scaled = scaled[panel_ids]
    panel_sq = squares[panel_ids]
    diagonal = kernel_block(panel_scaled, panel_sq, panel_scaled, panel_sq) + jnp.diag(extras[panel_ids])
    lower = jnp.linalg.cholesky(diagonal)
    block_scaled = scaled.reshape(N_ROW, R_DEV, EMBED)
    block_sq = squares.reshape(N_ROW, R_DEV)
    block_extra = extras.reshape(N_ROW, R_DEV)

    def factor_rows(index):
        rows = kernel_block(block_scaled[index], block_sq[index], panel_scaled, panel_sq)
        identity = index * R_DEV + jnp.arange(R_DEV, dtype=jnp.int32)
        rows = rows + jnp.where(identity[:, None] == panel_ids[None, :], block_extra[index][:, None], 0.0)
        return lax.linalg.triangular_solve(lower, rows, left_side=False, lower=True, transpose_a=True)
    factor_all = lax.map(factor_rows, jnp.arange(N_ROW, dtype=jnp.int32))

    def trailing_rows(index):
        pieces = []
        for stop in range(STOPS):
            visit = (index - stop) % N_ROW
            tile = kernel_block(block_scaled[index], block_sq[index], block_scaled[visit], block_sq[visit])
            tile = tile - jnp.dot(factor_all[index], factor_all[visit].T, precision=lax.Precision.HIGHEST)
            if stop == 0:
                tile = tile + jnp.diag(block_extra[index])
            pieces.append(tile.reshape(R_DEV, N_COL, SLICE))
        return jnp.stack(pieces, axis=2).reshape(R_DEV, N_COL * STOPS * SLICE)
    trailing = lax.map(trailing_rows, jnp.arange(N_ROW, dtype=jnp.int32)).reshape(CANDIDATES, STOPS * R_DEV)
    return (trailing, factor_all.reshape(CANDIDATES, PANEL))
```

```python
import functools

import jax
import jax.numpy as jnp
from jax import lax
from jax.experimental import pallas as pl
from jax.experimental.pallas import tpu as pltpu
from jax.sharding import PartitionSpec as P

PANEL = 1024
STOPS = 4
LEAF = 128
AHEAD = 4
F32 = jnp.float32
BF16 = jnp.bfloat16


def halves(x):
    high = x.astype(BF16)
    return high, (x - high.astype(F32)).astype(BF16)


def dot(a, b):
    return jnp.dot(a, b, preferred_element_type=F32)


def dot_nt(a, b):
    return lax.dot_general(a, b, (((1,), (1,)), ((), ())), preferred_element_type=F32)


def leaf_factor(tile, out_ref):
    n = LEAF
    groups = n // 8
    lane = lax.broadcasted_iota(jnp.int32, (8, 128), 1)
    rows = [tile[8 * i : 8 * i + 8, :] for i in range(groups)]

    def column(i, k):
        return jnp.broadcast_to(rows[i][:, k : k + 1], (8, 128))

    def one_row(x, r):
        return jnp.broadcast_to(x[r : r + 1, :], (8, 128))

    pending = [[column(i, k) for i in range(groups)] for k in range(AHEAD)]
    for k in range(n):
        g, r = divmod(k, 8)
        current = pending.pop(0)
        scale = lax.rsqrt(one_row(current[g], r))
        c = [current[i] * scale if i >= g else None for i in range(groups)]
        if k + AHEAD < n:
            pending.append([column(i, k + AHEAD) if i >= (k + AHEAD) // 8 else None for i in range(groups)])
        for j in range(len(pending)):
            gp, rp = divmod(k + 1 + j, 8)
            s = one_row(c[gp], rp)
            pending[j] = [pending[j][i] - c[i] * s if i >= gp else None for i in range(groups)]
        u = jnp.where(lane == k, scale, one_row(rows[g], r) * scale)
        out_ref[k : k + 1, :] = u[0:1, :]
        for i in range(g, groups):
            rows[i] = jnp.where(lane == k, 0.0, rows[i]) - c[i] * u


def count_kernel(base, matches_ref, out_ref, hits):
    first = base()

    def step(i, unused):
        ids = [first + 4 * i + q for q in range(4)]
        totals = [jnp.zeros((8, 128), F32) for q in range(4)]
        for block in range(matches_ref.shape[0] // 8):
            values = matches_ref[8 * block : 8 * block + 8, :]
            for q in range(4):
                totals[q] = totals[q] + jnp.where(values == ids[q], 1.0, 0.0)
        for q in range(4):
            hits[pl.ds(4 * i + q, 1), :] = jnp.sum(totals[q], axis=0, keepdims=True)
        return unused

    lax.fori_loop(0, 32, step, 0)
    out_ref[...] = jnp.broadcast_to(jnp.sum(hits[...].T, axis=0, keepdims=True), (8, 128))


def match_counts(matches):
    def base():
        return (lax.axis_index("row") * lax.axis_size("col") + lax.axis_index("col")) * LEAF

    return pl.pallas_call(
        functools.partial(count_kernel, base),
        out_shape=jax.ShapeDtypeStruct((8, 128), F32),
        in_specs=[pl.BlockSpec(memory_space=pltpu.VMEM)],
        out_specs=pl.BlockSpec(memory_space=pltpu.VMEM),
        scratch_shapes=[pltpu.VMEM((128, 128), F32)],
        name="match_counts",
    )(matches)


def squares_column(x_ref, start, count, chunk=128):
    parts = []
    for i in range(count // chunk):
        v = x_ref[start + i * chunk : start + (i + 1) * chunk, :].astype(F32)
        parts.append(jnp.sum(v * v, axis=1, keepdims=True))
    return parts


def to_lanes(column):
    return jnp.broadcast_to(column, (128, 128)).T[0:1, :]


def chain_kernel(panel_ref, extra_ref, xh_ref, xl_ref, sq_ref, a, leaf, low, sq_col):
    count = PANEL // LEAF
    for i in range(count):
        v = panel_ref[i * LEAF : (i + 1) * LEAF, :].astype(F32)
        s = jnp.sum(v * v, axis=1, keepdims=True)
        sq_col[i * LEAF : (i + 1) * LEAF, :] = jnp.broadcast_to(s, (LEAF, 128))
        sq_ref[0:1, i * LEAF : (i + 1) * LEAF] = to_lanes(s)
    row = lax.broadcasted_iota(jnp.int32, (PANEL, 256), 0)
    lane = lax.broadcasted_iota(jnp.int32, (PANEL, 256), 1)

    def build(n, unused):
        cols = pl.ds(pl.multiple_of(n * 256, 256), 256)
        g = dot_nt(panel_ref[...], panel_ref[cols, :])
        s = sq_col[...]
        k = jnp.exp(-0.5 * (jnp.concatenate([s, s], axis=1) + sq_ref[0:1, cols] - 2.0 * g))
        a[:, cols] = k + jnp.where(row == lane + n * 256, extra_ref[0:1, cols], 0.0)
        return unused

    lax.fori_loop(0, PANEL // 256, build, 0)
    r128 = lax.broadcasted_iota(jnp.int32, (LEAF, LEAF), 0)
    c128 = lax.broadcasted_iota(jnp.int32, (LEAF, LEAF), 1)

    def step(k, unused):
        own = pl.ds(pl.multiple_of(k * LEAF, LEAF), LEAF)
        leaf_factor(a[own, own], leaf)
        w = jnp.where(r128 >= c128, leaf[...], 0.0)
        wt = w.T
        wh, wl = halves(w)
        th, tl = halves(wt)
        w3 = jnp.concatenate([wh, wh, wl], axis=1)
        t3 = jnp.concatenate([th, tl, th], axis=0)
        ch, cl = halves(a[:, own])
        lcol = dot(jnp.concatenate([ch, ch, cl], axis=1), t3)
        a[:, own] = lcol
        a[own, own] = wt
        lh, ll = halves(lcol)
        low[:, 0:LEAF] = lh
        low[:, LEAF : 2 * LEAF] = lh
        low[:, 2 * LEAF :] = ll
        low[own, 0:LEAF] = th
        low[own, LEAF : 2 * LEAF] = th
        low[own, 2 * LEAF :] = tl

        def update(j, unused):
            cols = pl.ds(pl.multiple_of(j * LEAF, LEAF), LEAF)
            rh, rl = halves(a[own, cols])
            u = dot(w3, jnp.concatenate([rh, rl, rh], axis=0))
            uh, ul = halves(u)
            a[own, cols] = jnp.zeros((LEAF, LEAF), F32)
            a[:, cols] = a[:, cols] - dot(low[...], jnp.concatenate([uh, ul, uh], axis=0))
            return unused

        lax.fori_loop(k + 1, count, update, 0)
        return unused

    lax.fori_loop(0, count, step, 0)

    def finish(k, unused):
        own = pl.ds(pl.multiple_of(k * LEAF, LEAF), LEAF)
        row = lax.broadcasted_iota(jnp.int32, (PANEL, LEAF), 0)
        value = jnp.where(row < (k + 1) * LEAF, a[:, own], 0.0)
        high, lo = halves(value)
        xh_ref[:, own] = high
        xl_ref[:, own] = lo
        return unused

    lax.fori_loop(0, count, finish, 0)


def chain(panel, extras):
    vmem = pl.BlockSpec(memory_space=pltpu.VMEM)
    return pl.pallas_call(
        chain_kernel,
        out_shape=(
            jax.ShapeDtypeStruct((PANEL, PANEL), BF16),
            jax.ShapeDtypeStruct((PANEL, PANEL), BF16),
            jax.ShapeDtypeStruct((1, PANEL), F32),
        ),
        in_specs=[vmem, vmem],
        out_specs=(vmem, vmem, vmem),
        scratch_shapes=[
            pltpu.VMEM((PANEL, PANEL), F32),
            pltpu.VMEM((LEAF, LEAF), F32),
            pltpu.VMEM((PANEL, 3 * LEAF), BF16),
            pltpu.VMEM((PANEL, 128), F32),
        ],
        compiler_params=pltpu.CompilerParams(vmem_limit_bytes=60 << 20),
        cost_estimate=pl.CostEstimate(flops=100_000_000_000, bytes_accessed=10_000_000, transcendentals=0),
        name="panel_chain",
    )(panel, extras)


def trail_kernel(
    block_ref, own_ref, v1_ref, v2_ref, v3_ref, panel_ref, xh_ref, xl_ref, psq_ref, pextra_ref, extra_ref,
    trail_ref, factor_ref, rows, sq_col, sq_row, kh, kl, fh, fl, vh, vl,
):
    me = lax.axis_index("row")
    slot = lax.axis_index("col")
    row_count = lax.axis_size("row")
    total = 1024 + 3 * LEAF
    rows[0:1024, :] = block_ref[...]
    for s, ref in enumerate((v1_ref, v2_ref, v3_ref)):
        rows[1024 + s * LEAF : 1024 + (s + 1) * LEAF, :] = ref[...]

    def squares(i, unused):
        at = pl.ds(pl.multiple_of(i * LEAF, LEAF), LEAF)
        v = rows[at, :].astype(F32)
        s = jnp.sum(v * v, axis=1, keepdims=True)
        sq_col[at, :] = jnp.broadcast_to(s, (LEAF, 128))
        return unused

    lax.fori_loop(0, total // LEAF, squares, 0)
    own = pl.ds(pl.multiple_of(slot * LEAF, LEAF), LEAF)
    sq_row[0:1, 0:128] = sq_col[own, :].T[0:1, :]
    for s in range(3):
        sq_row[0:1, (s + 1) * LEAF : (s + 2) * LEAF] = sq_col[1024 + s * LEAF : 1024 + (s + 1) * LEAF, :].T[0:1, :]

    lead_row = lax.broadcasted_iota(jnp.int32, (32, 256), 0)
    lead_lane = lax.broadcasted_iota(jnp.int32, (32, 256), 1)

    def kernel_part(n, unused):
        cols = pl.ds(pl.multiple_of(n * 256, 256), 256)
        g = dot_nt(rows[...], panel_ref[cols, :])
        s = sq_col[...]
        k = jnp.exp(-0.5 * (jnp.concatenate([s, s], axis=1) + psq_ref[0:1, cols] - 2.0 * g))
        high, lo = halves(k)
        kh[:, cols] = high
        kl[:, cols] = lo
        extra = pextra_ref[0:1, cols]

        def fix(start, block, scale):
            part = k[start : start + 32, :]
            hit = lead_lane + n * 256 == block * 32 + lead_row
            part = part + jnp.where(hit, extra * scale, 0.0)
            high, lo = halves(part)
            kh[start : start + 32, cols] = high
            kl[start : start + 32, cols] = lo

        fix(0, me, 1.0)
        lead = jnp.where(slot == 0, 1.0, 0.0).astype(F32)
        for s in range(3):
            fix(1024 + s * LEAF, lax.rem(me + row_count - s - 1, row_count), lead)
        return unused

    lax.fori_loop(0, PANEL // 256, kernel_part, 0)
    for n in range(4):
        depth = 256 * (n + 1)
        cols = slice(256 * n, 256 * n + 256)
        f = dot(kh[:, :depth], xh_ref[:depth, cols])
        f = f + dot(kh[:, :depth], xl_ref[:depth, cols])
        f = f + dot(kl[:, :depth], xh_ref[:depth, cols])
        high, lo = halves(f)
        fh[:, cols] = high
        fl[:, cols] = lo
    factor_ref[...] = fh[own, :].astype(F32) + fl[own, :].astype(F32)
    vh[0:LEAF, :] = fh[own, :]
    vl[0:LEAF, :] = fl[own, :]
    vh[LEAF:, :] = fh[1024:, :]
    vl[LEAF:, :] = fl[1024:, :]
    r = lax.broadcasted_iota(jnp.int32, (256, LEAF), 0)
    c = lax.broadcasted_iota(jnp.int32, (256, LEAF), 1)

    def tile(i, unused):
        at = pl.ds(pl.multiple_of(i * 256, 256), 256)
        left = rows[at, :]
        g = jnp.concatenate([dot_nt(left, rows[own, :]), dot_nt(left, rows[1024:, :])], axis=1)
        s = sq_col[at, :]
        k = jnp.exp(-0.5 * (jnp.concatenate([s] * 4, axis=1) + sq_row[...] - 2.0 * g))
        ff = dot_nt(fh[at, :], vh[...])
        ff = ff + dot_nt(fh[at, :], vl[...])
        ff = ff + dot_nt(fl[at, :], vh[...])
        t = k - ff
        trail_ref[at, :] = t
        diagonal = jnp.where(r + i * 256 == c + slot * LEAF, extra_ref[0:1, :], 0.0)
        trail_ref[at, 0:LEAF] = t[:, 0:LEAF] + diagonal
        return unused

    lax.fori_loop(0, 4, tile, 0)


def trail(block, own, visitors, panel, xh, xl, psq, pextra, extra):
    vmem = pl.BlockSpec(memory_space=pltpu.VMEM)
    total = 1024 + 3 * LEAF
    return pl.pallas_call(
        trail_kernel,
        out_shape=(
            jax.ShapeDtypeStruct((1024, STOPS * LEAF), F32),
            jax.ShapeDtypeStruct((LEAF, PANEL), F32),
        ),
        in_specs=[vmem] * 11,
        out_specs=(vmem, vmem),
        scratch_shapes=[
            pltpu.VMEM((total, 2048), BF16),
            pltpu.VMEM((total, 128), F32),
            pltpu.VMEM((1, STOPS * LEAF), F32),
            pltpu.VMEM((total, PANEL), BF16),
            pltpu.VMEM((total, PANEL), BF16),
            pltpu.VMEM((total, PANEL), BF16),
            pltpu.VMEM((total, PANEL), BF16),
            pltpu.VMEM((STOPS * LEAF, PANEL), BF16),
            pltpu.VMEM((STOPS * LEAF, PANEL), BF16),
        ],
        compiler_params=pltpu.CompilerParams(vmem_limit_bytes=60 << 20),
        cost_estimate=pl.CostEstimate(flops=30_000_000_000, bytes_accessed=20_000_000, transcendentals=0),
        name="trailing",
    )(block, own, *visitors, panel, xh, xl, psq, pextra, extra)


def body(embeddings, inverse_scales, matches):
    row_count = lax.axis_size("row")
    share = PANEL // row_count
    scaled = (embeddings.astype(F32) * inverse_scales[None, :]).astype(BF16)
    pairs = matches.reshape(-1, 128, 2).transpose(0, 2, 1).reshape(-1, 128)
    counts = match_counts(pairs)
    extra = 0.1 + 0.5 * counts
    c0 = counts[0, :share].astype(jnp.int32)
    digits = jnp.stack([c0 % 256, (c0 // 256) % 256, c0 // 65536], axis=1).astype(F32).astype(BF16)
    digits = jnp.pad(digits, ((0, 0), (0, 125)))
    lead = jnp.concatenate([scaled[:share], digits], axis=1)
    lead = lax.all_gather(lead, "col")[0]
    panel = lax.all_gather(lead, "row", axis=0, tiled=True)
    d = panel[:, 2048:2051].astype(F32)
    panel_extra = (0.1 + 0.5 * (d[:, 0] + 256.0 * d[:, 1] + 65536.0 * d[:, 2]))[None, :]
    panel = panel[:, :2048]
    block = lax.all_gather(scaled, "col", axis=0, tiled=True)
    visitors = [
        lax.ppermute(scaled, "row", [((i - s) % row_count, i) for i in range(row_count)])
        for s in range(1, STOPS)
    ]
    xh, xl, psq = chain(panel, panel_extra)
    return trail(block, scaled, visitors, panel, xh, xl, psq, panel_extra, extra)


def solution(mesh):
    return jax.shard_map(
        body,
        mesh=mesh,
        in_specs=(P(("row", "col"), None), P(), P()),
        out_specs=(P("row", "col"), P(("row", "col"), None)),
        check_vma=False,
    )
```

```python
import functools

import jax
import jax.numpy as jnp
from jax import lax
from jax.experimental import pallas as pl
from jax.experimental.pallas import tpu as pltpu
from jax.sharding import PartitionSpec as P

PANEL = 1024
STOPS = 4
LEAF = 128
AHEAD = 4
F32 = jnp.float32
BF16 = jnp.bfloat16


def halves(x):
    high = x.astype(BF16)
    return high, (x - high.astype(F32)).astype(BF16)


def dot(a, b):
    return jnp.dot(a, b, preferred_element_type=F32)


def dot_nt(a, b):
    return lax.dot_general(a, b, (((1,), (1,)), ((), ())), preferred_element_type=F32)


def leaf_factor(tile, out_ref):
    n = LEAF
    groups = n // 8
    lane = lax.broadcasted_iota(jnp.int32, (8, 128), 1)
    rows = [tile[8 * i : 8 * i + 8, :] for i in range(groups)]

    def column(i, k):
        return jnp.broadcast_to(rows[i][:, k : k + 1], (8, 128))

    def one_row(x, r):
        return jnp.broadcast_to(x[r : r + 1, :], (8, 128))

    pending = [[column(i, k) for i in range(groups)] for k in range(AHEAD)]
    for k in range(n):
        g, r = divmod(k, 8)
        current = pending.pop(0)
        scale = lax.rsqrt(one_row(current[g], r))
        c = [current[i] * scale if i >= g else None for i in range(groups)]
        if k + AHEAD < n:
            pending.append([column(i, k + AHEAD) if i >= (k + AHEAD) // 8 else None for i in range(groups)])
        for j in range(len(pending)):
            gp, rp = divmod(k + 1 + j, 8)
            s = one_row(c[gp], rp)
            pending[j] = [pending[j][i] - c[i] * s if i >= gp else None for i in range(groups)]
        u = jnp.where(lane == k, scale, one_row(rows[g], r) * scale)
        out_ref[k : k + 1, :] = u[0:1, :]
        for i in range(g, groups):
            rows[i] = jnp.where(lane == k, 0.0, rows[i]) - c[i] * u


MESH = pl.DeviceIdType.MESH
SIDE = 4


def counts_step(values, first):
    sub32 = lax.broadcasted_iota(jnp.int32, (32, 128), 0)
    sub16 = lax.broadcasted_iota(jnp.int32, (16, 128), 0)
    place = jnp.where((values & 1023) < 32, values & 31, -1)
    inside = values - first
    part = jnp.where((inside >= 0) & (inside < 128), inside >> 4, -1)
    left = jnp.concatenate(
        [jnp.where(sub32 == values >> 10, 1.0, 0.0), jnp.where(sub16 == part, 1.0, 0.0)], axis=0
    ).astype(BF16)
    right = jnp.concatenate(
        [jnp.where(sub32 == place, 1.0, 0.0), jnp.where(sub16 == (values & 15), 1.0, 0.0)], axis=0
    ).astype(BF16)
    return left, right


def spread(table, width):
    n = table.shape[0]
    total = n * width
    tiled = jnp.concatenate([table] * n, axis=1)
    row = lax.broadcasted_iota(jnp.int32, (n, total), 0)
    lane = lax.broadcasted_iota(jnp.int32, (n, total), 1)
    return jnp.sum(jnp.where(lane >> (width.bit_length() - 1) == row, tiled, 0.0), axis=0, keepdims=True)


def gather_kernel(
    emb_ref, inv_ref, pairs_ref, scaled_ref, panel, pextra_ref, extra_ref, hits, zs, zr, ss, sr, cs, cr,
):
    me = lax.axis_index("row")
    slot = lax.axis_index("col")
    x, y, core = me // 8, (me // 2) % SIDE, me % 2
    xp, xm, xo = (x + 1) % SIDE, (x + 3) % SIDE, (x + 2) % SIDE
    yp, ym, yo = (y + 1) % SIDE, (y + 3) % SIDE, (y + 2) % SIDE

    def row_at(x, y, core):
        return (x * SIDE + y) * 2 + core

    to_xp, to_xm = row_at(xp, y, core), row_at(xm, y, core)
    to_yp, to_ym = row_at(x, yp, core), row_at(x, ym, core)
    twin = row_at(x, y, 1 - core)
    barrier = pltpu.get_barrier_semaphore()
    for other in (to_xp, to_xm, to_yp, to_ym, twin):
        pl.semaphore_signal(barrier, inc=1, device_id=(other, slot), device_id_type=MESH)
    for j in range(1, 8):
        pl.semaphore_signal(barrier, inc=1, device_id=(me, (slot + j) % 8), device_id_type=MESH)

    def scale(start, count):
        v = emb_ref[start : start + count, :].astype(F32) * inv_ref[0:1, :]
        scaled_ref[start : start + count, :] = v.astype(BF16)

    scale(0, 32)

    @pl.when(slot == 0)
    def _():
        panel[x, y, core] = scaled_ref[0:32, :]

    pl.semaphore_wait(barrier, 12)

    def copy(view, row, col, send, recv):
        return pltpu.make_async_remote_copy(
            src_ref=view, dst_ref=view, send_sem=send, recv_sem=recv, device_id=(row, col), device_id_type=MESH
        )

    def chunk(q):
        return panel.at[x, y, core, :, pl.ds(pl.multiple_of(q * 256, 256), 256)]

    @pl.when(slot == 0)
    def _():
        for c in range(1, 8):
            copy(chunk(c), me, c, zs.at[c], zr.at[c]).start()
        for c in range(1, 8):
            copy(chunk(0), me, c, zs.at[7 + c], zr.at[0]).start()

    scale(32, 96)

    @pl.when(slot != 0)
    def _():
        copy(chunk(slot), me, slot, zs.at[0], zr.at[slot]).wait_recv()
        for j in range(1, 8):
            other = (slot + j) % 8

            @pl.when(other != 0)
            def _(other=other, j=j):
                copy(chunk(slot), me, other, zs.at[j], zr.at[slot]).start()

    first = row_at(x, y, core) * 1024 + slot * 128

    def count(i, total):
        lefts, rights = [], []
        for r in range(8):
            left, right = counts_step(jnp.broadcast_to(pairs_ref[pl.ds(i * 8 + r, 1), :], (8, 128))[0:1, :], first)
            lefts.append(left)
            rights.append(right)
        return total + dot_nt(jnp.concatenate(lefts, axis=1), jnp.concatenate(rights, axis=1))

    hits[:, 0:48] = lax.fori_loop(0, pairs_ref.shape[0] // 8, count, jnp.zeros((48, 48), F32))

    @pl.when(slot != 0)
    def _():
        for j in range(1, 8):
            other = (slot + j) % 8
            copy(chunk(other), me, slot, zs.at[0], zr.at[other]).wait_recv()

    near, far = pl.ds(0, 1024), pl.ds(1024, 1024)
    sent = []

    def send(view, row, i):
        c = copy(view, row, slot, ss.at[i], sr.at[i])
        c.start()
        sent.append(c)

    def arrive(view, i):
        copy(view, twin, slot, ss.at[i], sr.at[i]).wait_recv()

    passed = []

    def share(view, back, i):
        c = copy(view, twin, slot, cs.at[i], cr.at[i])
        c.start()
        passed.append((c, back, i))

    own_near, own_far = panel.at[x, y, core, :, near], panel.at[x, y, core, :, far]
    send(own_near, to_xp, 0)
    send(own_far, to_yp, 1)
    send(own_near, to_xm, 2)
    send(own_far, to_ym, 3)
    share(panel.at[x, y, core], panel.at[x, y, 1 - core], 0)
    top, low = pl.ds(0, 16), pl.ds(16, 16)
    arrive(panel.at[xm, y, core, :, near], 0)
    send(panel.at[xm, y, core, top, near], to_xp, 4)
    arrive(panel.at[x, ym, core, :, far], 1)
    send(panel.at[x, ym, core, top, far], to_yp, 5)
    arrive(panel.at[xp, y, core, :, near], 2)
    send(panel.at[xp, y, core, low, near], to_xm, 6)
    arrive(panel.at[x, yp, core, :, far], 3)
    send(panel.at[x, yp, core, low, far], to_ym, 7)
    share(panel.at[xm, y, core, :, near], panel.at[xm, y, 1 - core, :, near], 1)
    share(panel.at[x, ym, core, :, far], panel.at[x, ym, 1 - core, :, far], 2)
    share(panel.at[xp, y, core, :, near], panel.at[xp, y, 1 - core, :, near], 3)
    share(panel.at[x, yp, core, :, far], panel.at[x, yp, 1 - core, :, far], 4)
    arrive(panel.at[xo, y, core, top, near], 4)
    arrive(panel.at[xo, y, core, low, near], 6)
    send(panel.at[:, y, core, :, near], to_yp, 8)
    send(panel.at[:, y, core, :, near], to_ym, 10)
    arrive(panel.at[x, yo, core, top, far], 5)
    arrive(panel.at[x, yo, core, low, far], 7)
    send(panel.at[x, :, core, :, far], to_xp, 9)
    send(panel.at[x, :, core, :, far], to_xm, 11)
    share(panel.at[xo, y, core, :, near], panel.at[xo, y, 1 - core, :, near], 5)
    share(panel.at[x, yo, core, :, far], panel.at[x, yo, 1 - core, :, far], 6)

    row_hits = hits[:, 0:48]
    pextra_ref[...] = 0.1 + 0.5 * spread(row_hits[0:32, 0:32], 32)
    extra_ref[...] = 0.1 + 0.5 * spread(row_hits[32:40, 32:48], 16)

    first_two, last_two = pl.ds(0, 2), pl.ds(2, 2)
    arrive(panel.at[:, ym, core, :, near], 8)
    send(panel.at[first_two, ym, core, :, near], to_yp, 12)
    arrive(panel.at[xm, :, core, :, far], 9)
    send(panel.at[xm, first_two, core, :, far], to_xp, 13)
    arrive(panel.at[:, yp, core, :, near], 10)
    send(panel.at[last_two, yp, core, :, near], to_ym, 14)
    arrive(panel.at[xp, :, core, :, far], 11)
    send(panel.at[xp, last_two, core, :, far], to_xm, 15)
    share(panel.at[:, ym, core, :, near], panel.at[:, ym, 1 - core, :, near], 7)
    share(panel.at[xm, :, core, :, far], panel.at[xm, :, 1 - core, :, far], 8)
    share(panel.at[:, yp, core, :, near], panel.at[:, yp, 1 - core, :, near], 9)
    share(panel.at[xp, :, core, :, far], panel.at[xp, :, 1 - core, :, far], 10)
    arrive(panel.at[first_two, yo, core, :, near], 12)
    arrive(panel.at[last_two, yo, core, :, near], 14)
    share(panel.at[:, yo, core, :, near], panel.at[:, yo, 1 - core, :, near], 11)
    arrive(panel.at[xo, first_two, core, :, far], 13)
    arrive(panel.at[xo, last_two, core, :, far], 15)
    share(panel.at[xo, :, core, :, far], panel.at[xo, :, 1 - core, :, far], 12)
    for c, back, i in passed:
        copy(back, twin, slot, cs.at[i], cr.at[i]).wait_recv()
        c.wait_send()
    for c in sent:
        c.wait_send()

    @pl.when(slot == 0)
    def _():
        for c in range(1, 8):
            copy(chunk(c), me, c, zs.at[c], zr.at[c]).wait_send()
            copy(chunk(0), me, c, zs.at[7 + c], zr.at[0]).wait_send()

    @pl.when(slot != 0)
    def _():
        for j in range(1, 8):
            other = (slot + j) % 8

            @pl.when(other != 0)
            def _(other=other, j=j):
                copy(chunk(slot), me, other, zs.at[j], zr.at[slot]).wait_send()


def gather_panel(embeddings, inverse_scales, pairs):
    vmem = pl.BlockSpec(memory_space=pltpu.VMEM)
    return pl.pallas_call(
        gather_kernel,
        out_shape=(
            jax.ShapeDtypeStruct((LEAF, 2048), BF16),
            jax.ShapeDtypeStruct((SIDE, SIDE, 2, 32, 2048), BF16),
            jax.ShapeDtypeStruct((1, PANEL), F32),
            jax.ShapeDtypeStruct((1, LEAF), F32),
        ),
        in_specs=[vmem] * 3,
        out_specs=(vmem,) * 4,
        scratch_shapes=[
            pltpu.VMEM((48, 128), F32),
            pltpu.SemaphoreType.DMA((15,)),
            pltpu.SemaphoreType.DMA((8,)),
            pltpu.SemaphoreType.DMA((16,)),
            pltpu.SemaphoreType.DMA((16,)),
            pltpu.SemaphoreType.DMA((13,)),
            pltpu.SemaphoreType.DMA((13,)),
        ],
        compiler_params=pltpu.CompilerParams(
            collective_id=0, has_side_effects=True, vmem_limit_bytes=40 << 20
        ),
        name="panel_gather",
    )(embeddings, inverse_scales, pairs)


def to_lanes(column):
    return jnp.broadcast_to(column, (128, 128)).T[0:1, :]


def chain_kernel(panel_ref, extra_ref, xh_ref, xl_ref, sq_ref, a, leaf, low, sq_col):
    count = PANEL // LEAF
    for i in range(count):
        v = panel_ref[i * LEAF : (i + 1) * LEAF, :].astype(F32)
        s = jnp.sum(v * v, axis=1, keepdims=True)
        sq_col[i * LEAF : (i + 1) * LEAF, :] = jnp.broadcast_to(s, (LEAF, 128))
        sq_ref[0:1, i * LEAF : (i + 1) * LEAF] = to_lanes(s)
    row = lax.broadcasted_iota(jnp.int32, (PANEL, 256), 0)
    lane = lax.broadcasted_iota(jnp.int32, (PANEL, 256), 1)

    def build(n, unused):
        cols = pl.ds(pl.multiple_of(n * 256, 256), 256)
        g = dot_nt(panel_ref[...], panel_ref[cols, :])
        s = sq_col[...]
        k = jnp.exp(-0.5 * (jnp.concatenate([s, s], axis=1) + sq_ref[0:1, cols] - 2.0 * g))
        a[:, cols] = k + jnp.where(row == lane + n * 256, extra_ref[0:1, cols], 0.0)
        return unused

    lax.fori_loop(0, PANEL // 256, build, 0)
    r128 = lax.broadcasted_iota(jnp.int32, (LEAF, LEAF), 0)
    c128 = lax.broadcasted_iota(jnp.int32, (LEAF, LEAF), 1)

    def step(k, unused):
        own = pl.ds(pl.multiple_of(k * LEAF, LEAF), LEAF)
        leaf_factor(a[own, own], leaf)
        w = jnp.where(r128 >= c128, leaf[...], 0.0)
        wt = w.T
        wh, wl = halves(w)
        th, tl = halves(wt)
        w3 = jnp.concatenate([wh, wh, wl], axis=1)
        t3 = jnp.concatenate([th, tl, th], axis=0)
        ch, cl = halves(a[:, own])
        lcol = dot(jnp.concatenate([ch, ch, cl], axis=1), t3)
        a[:, own] = lcol
        a[own, own] = wt
        lh, ll = halves(lcol)
        low[:, 0:LEAF] = lh
        low[:, LEAF : 2 * LEAF] = lh
        low[:, 2 * LEAF :] = ll
        low[own, 0:LEAF] = th
        low[own, LEAF : 2 * LEAF] = th
        low[own, 2 * LEAF :] = tl

        def update(j, unused):
            cols = pl.ds(pl.multiple_of(j * LEAF, LEAF), LEAF)
            rh, rl = halves(a[own, cols])
            u = dot(w3, jnp.concatenate([rh, rl, rh], axis=0))
            uh, ul = halves(u)
            a[own, cols] = jnp.zeros((LEAF, LEAF), F32)
            a[:, cols] = a[:, cols] - dot(low[...], jnp.concatenate([uh, ul, uh], axis=0))
            return unused

        lax.fori_loop(k + 1, count, update, 0)
        return unused

    lax.fori_loop(0, count, step, 0)

    def finish(k, unused):
        own = pl.ds(pl.multiple_of(k * LEAF, LEAF), LEAF)
        row = lax.broadcasted_iota(jnp.int32, (PANEL, LEAF), 0)
        value = jnp.where(row < (k + 1) * LEAF, a[:, own], 0.0)
        high, lo = halves(value)
        xh_ref[:, own] = high
        xl_ref[:, own] = lo
        return unused

    lax.fori_loop(0, count, finish, 0)


def chain(panel, extras):
    vmem = pl.BlockSpec(memory_space=pltpu.VMEM)
    return pl.pallas_call(
        chain_kernel,
        out_shape=(
            jax.ShapeDtypeStruct((PANEL, PANEL), BF16),
            jax.ShapeDtypeStruct((PANEL, PANEL), BF16),
            jax.ShapeDtypeStruct((1, PANEL), F32),
        ),
        in_specs=[vmem, vmem],
        out_specs=(vmem, vmem, vmem),
        scratch_shapes=[
            pltpu.VMEM((PANEL, PANEL), F32),
            pltpu.VMEM((LEAF, LEAF), F32),
            pltpu.VMEM((PANEL, 3 * LEAF), BF16),
            pltpu.VMEM((PANEL, 128), F32),
        ],
        compiler_params=pltpu.CompilerParams(vmem_limit_bytes=60 << 20),
        cost_estimate=pl.CostEstimate(flops=100_000_000_000, bytes_accessed=10_000_000, transcendentals=0),
        name="panel_chain",
    )(panel, extras)


def trail_kernel(
    block_ref, own_ref, v1_ref, v2_ref, v3_ref, panel_ref, xh_ref, xl_ref, psq_ref, pextra_ref, extra_ref,
    trail_ref, factor_ref, rows, sq_col, sq_row, kh, kl, fh, fl, vh, vl,
):
    me = lax.axis_index("row")
    slot = lax.axis_index("col")
    row_count = lax.axis_size("row")
    total = 1024 + 3 * LEAF
    rows[0:1024, :] = block_ref[...]
    for s, ref in enumerate((v1_ref, v2_ref, v3_ref)):
        rows[1024 + s * LEAF : 1024 + (s + 1) * LEAF, :] = ref[...]

    def squares(i, unused):
        at = pl.ds(pl.multiple_of(i * LEAF, LEAF), LEAF)
        v = rows[at, :].astype(F32)
        s = jnp.sum(v * v, axis=1, keepdims=True)
        sq_col[at, :] = jnp.broadcast_to(s, (LEAF, 128))
        return unused

    lax.fori_loop(0, total // LEAF, squares, 0)
    own = pl.ds(pl.multiple_of(slot * LEAF, LEAF), LEAF)
    sq_row[0:1, 0:128] = sq_col[own, :].T[0:1, :]
    for s in range(3):
        sq_row[0:1, (s + 1) * LEAF : (s + 2) * LEAF] = sq_col[1024 + s * LEAF : 1024 + (s + 1) * LEAF, :].T[0:1, :]

    lead_row = lax.broadcasted_iota(jnp.int32, (32, 256), 0)
    lead_lane = lax.broadcasted_iota(jnp.int32, (32, 256), 1)

    def kernel_part(n, unused):
        cols = pl.ds(pl.multiple_of(n * 256, 256), 256)
        g = dot_nt(rows[...], panel_ref[cols, :])
        s = sq_col[...]
        k = jnp.exp(-0.5 * (jnp.concatenate([s, s], axis=1) + psq_ref[0:1, cols] - 2.0 * g))
        high, lo = halves(k)
        kh[:, cols] = high
        kl[:, cols] = lo
        extra = pextra_ref[0:1, cols]

        def fix(start, block, scale):
            part = k[start : start + 32, :]
            hit = lead_lane + n * 256 == block * 32 + lead_row
            part = part + jnp.where(hit, extra * scale, 0.0)
            high, lo = halves(part)
            kh[start : start + 32, cols] = high
            kl[start : start + 32, cols] = lo

        fix(0, me, 1.0)
        lead = jnp.where(slot == 0, 1.0, 0.0).astype(F32)
        for s in range(3):
            fix(1024 + s * LEAF, lax.rem(me + row_count - s - 1, row_count), lead)
        return unused

    lax.fori_loop(0, PANEL // 256, kernel_part, 0)
    for n in range(4):
        depth = 256 * (n + 1)
        cols = slice(256 * n, 256 * n + 256)
        f = dot(kh[:, :depth], xh_ref[:depth, cols])
        f = f + dot(kh[:, :depth], xl_ref[:depth, cols])
        f = f + dot(kl[:, :depth], xh_ref[:depth, cols])
        high, lo = halves(f)
        fh[:, cols] = high
        fl[:, cols] = lo
    factor_ref[...] = fh[own, :].astype(F32) + fl[own, :].astype(F32)
    vh[0:LEAF, :] = fh[own, :]
    vl[0:LEAF, :] = fl[own, :]
    vh[LEAF:, :] = fh[1024:, :]
    vl[LEAF:, :] = fl[1024:, :]
    r = lax.broadcasted_iota(jnp.int32, (256, LEAF), 0)
    c = lax.broadcasted_iota(jnp.int32, (256, LEAF), 1)

    def tile(i, unused):
        at = pl.ds(pl.multiple_of(i * 256, 256), 256)
        left = rows[at, :]
        g = jnp.concatenate([dot_nt(left, rows[own, :]), dot_nt(left, rows[1024:, :])], axis=1)
        s = sq_col[at, :]
        k = jnp.exp(-0.5 * (jnp.concatenate([s] * 4, axis=1) + sq_row[...] - 2.0 * g))
        ff = dot_nt(fh[at, :], vh[...])
        ff = ff + dot_nt(fh[at, :], vl[...])
        ff = ff + dot_nt(fl[at, :], vh[...])
        t = k - ff
        trail_ref[at, :] = t
        diagonal = jnp.where(r + i * 256 == c + slot * LEAF, extra_ref[0:1, :], 0.0)
        trail_ref[at, 0:LEAF] = t[:, 0:LEAF] + diagonal
        return unused

    lax.fori_loop(0, 4, tile, 0)


def trail(block, own, visitors, panel, xh, xl, psq, pextra, extra):
    vmem = pl.BlockSpec(memory_space=pltpu.VMEM)
    total = 1024 + 3 * LEAF
    return pl.pallas_call(
        trail_kernel,
        out_shape=(
            jax.ShapeDtypeStruct((1024, STOPS * LEAF), F32),
            jax.ShapeDtypeStruct((LEAF, PANEL), F32),
        ),
        in_specs=[vmem] * 11,
        out_specs=(vmem, vmem),
        scratch_shapes=[
            pltpu.VMEM((total, 2048), BF16),
            pltpu.VMEM((total, 128), F32),
            pltpu.VMEM((1, STOPS * LEAF), F32),
            pltpu.VMEM((total, PANEL), BF16),
            pltpu.VMEM((total, PANEL), BF16),
            pltpu.VMEM((total, PANEL), BF16),
            pltpu.VMEM((total, PANEL), BF16),
            pltpu.VMEM((STOPS * LEAF, PANEL), BF16),
            pltpu.VMEM((STOPS * LEAF, PANEL), BF16),
        ],
        compiler_params=pltpu.CompilerParams(vmem_limit_bytes=60 << 20),
        cost_estimate=pl.CostEstimate(flops=30_000_000_000, bytes_accessed=20_000_000, transcendentals=0),
        name="trailing",
    )(block, own, *visitors, panel, xh, xl, psq, pextra, extra)


def body(embeddings, inverse_scales, matches):
    row_count = lax.axis_size("row")
    pairs = matches.reshape(-1, 128, 2).transpose(0, 2, 1).reshape(-1, 128)
    scaled, panel, panel_extra, extra = gather_panel(embeddings, inverse_scales[None, :], pairs)
    panel = panel.reshape(PANEL, -1)
    block = lax.all_gather(scaled, "col", axis=0, tiled=True)
    visitors = [
        lax.ppermute(scaled, "row", [((i - s) % row_count, i) for i in range(row_count)])
        for s in range(1, STOPS)
    ]
    xh, xl, psq = chain(panel, panel_extra)
    return trail(block, scaled, visitors, panel, xh, xl, psq, panel_extra, extra)


def solution(mesh):
    return jax.shard_map(
        body,
        mesh=mesh,
        in_specs=(P(("row", "col"), None), P(), P()),
        out_specs=(P("row", "col"), P(("row", "col"), None)),
        check_vma=False,
    )
```

```python
import functools

import jax
import jax.numpy as jnp
from jax import lax
from jax.experimental import pallas as pl
from jax.experimental.pallas import tpu as pltpu
from jax.sharding import PartitionSpec as P

PANEL = 1024
STOPS = 4
LEAF = 128
AHEAD = 4
F32 = jnp.float32
BF16 = jnp.bfloat16


def halves(x):
    high = x.astype(BF16)
    return high, (x - high.astype(F32)).astype(BF16)


def dot(a, b):
    return jnp.dot(a, b, preferred_element_type=F32)


def dot_nt(a, b):
    return lax.dot_general(a, b, (((1,), (1,)), ((), ())), preferred_element_type=F32)


def leaf_factor(tile, out_ref):
    n = LEAF
    groups = n // 8
    lane = lax.broadcasted_iota(jnp.int32, (8, 128), 1)
    rows = [tile[8 * i : 8 * i + 8, :] for i in range(groups)]

    def column(i, k):
        return jnp.broadcast_to(rows[i][:, k : k + 1], (8, 128))

    def one_row(x, r):
        return jnp.broadcast_to(x[r : r + 1, :], (8, 128))

    pending = [[column(i, k) for i in range(groups)] for k in range(AHEAD)]
    for k in range(n):
        g, r = divmod(k, 8)
        current = pending.pop(0)
        scale = lax.rsqrt(one_row(current[g], r))
        c = [current[i] * scale if i >= g else None for i in range(groups)]
        if k + AHEAD < n:
            pending.append([column(i, k + AHEAD) if i >= (k + AHEAD) // 8 else None for i in range(groups)])
        for j in range(len(pending)):
            gp, rp = divmod(k + 1 + j, 8)
            s = one_row(c[gp], rp)
            pending[j] = [pending[j][i] - c[i] * s if i >= gp else None for i in range(groups)]
        u = jnp.where(lane == k, scale, one_row(rows[g], r) * scale)
        out_ref[k : k + 1, :] = u[0:1, :]
        for i in range(g, groups):
            rows[i] = jnp.where(lane == k, 0.0, rows[i]) - c[i] * u


MESH = pl.DeviceIdType.MESH
SIDE = 4


def counts_step(values, first):
    sub32 = lax.broadcasted_iota(jnp.int32, (32, 128), 0)
    sub16 = lax.broadcasted_iota(jnp.int32, (16, 128), 0)
    place = jnp.where((values & 1023) < 32, values & 31, -1)
    inside = values - first
    part = jnp.where((inside >= 0) & (inside < 128), inside >> 4, -1)
    left = jnp.concatenate(
        [jnp.where(sub32 == values >> 10, 1.0, 0.0), jnp.where(sub16 == part, 1.0, 0.0)], axis=0
    ).astype(BF16)
    right = jnp.concatenate(
        [jnp.where(sub32 == place, 1.0, 0.0), jnp.where(sub16 == (values & 15), 1.0, 0.0)], axis=0
    ).astype(BF16)
    return left, right


def spread(table, width):
    n = table.shape[0]
    total = n * width
    tiled = jnp.concatenate([table] * n, axis=1)
    row = lax.broadcasted_iota(jnp.int32, (n, total), 0)
    lane = lax.broadcasted_iota(jnp.int32, (n, total), 1)
    return jnp.sum(jnp.where(lane >> (width.bit_length() - 1) == row, tiled, 0.0), axis=0, keepdims=True)


def gather_kernel(
    emb_ref, inv_ref, pairs_ref, scaled_ref, panel, pextra_ref, extra_ref, hits, zs, zr, ss, sr, cs, cr,
):
    me = lax.axis_index("row")
    slot = lax.axis_index("col")
    x, y, core = me // 8, (me // 2) % SIDE, me % 2
    xp, xm, xo = (x + 1) % SIDE, (x + 3) % SIDE, (x + 2) % SIDE
    yp, ym, yo = (y + 1) % SIDE, (y + 3) % SIDE, (y + 2) % SIDE

    def row_at(x, y, core):
        return (x * SIDE + y) * 2 + core

    to_xp, to_xm = row_at(xp, y, core), row_at(xm, y, core)
    to_yp, to_ym = row_at(x, yp, core), row_at(x, ym, core)
    twin = row_at(x, y, 1 - core)
    barrier = pltpu.get_barrier_semaphore()
    for other in (to_xp, to_xm, to_yp, to_ym, twin):
        pl.semaphore_signal(barrier, inc=1, device_id=(other, slot), device_id_type=MESH)
    for j in range(1, 8):
        pl.semaphore_signal(barrier, inc=1, device_id=(me, (slot + j) % 8), device_id_type=MESH)

    def scale(start, count):
        v = emb_ref[start : start + count, :].astype(F32) * inv_ref[0:1, :]
        scaled_ref[start : start + count, :] = v.astype(BF16)

    scale(0, 32)

    @pl.when(slot == 0)
    def _():
        panel[x, y, core] = scaled_ref[0:32, :]

    pl.semaphore_wait(barrier, 12)

    def copy(view, row, col, send, recv):
        return pltpu.make_async_remote_copy(
            src_ref=view, dst_ref=view, send_sem=send, recv_sem=recv, device_id=(row, col), device_id_type=MESH
        )

    def chunk(q):
        return panel.at[x, y, core, :, pl.ds(pl.multiple_of(q * 256, 256), 256)]

    @pl.when(slot == 0)
    def _():
        for c in range(1, 8):
            copy(chunk(c), me, c, zs.at[c], zr.at[c]).start()
        for c in range(1, 8):
            copy(chunk(0), me, c, zs.at[7 + c], zr.at[0]).start()

    scale(32, 96)

    @pl.when(slot != 0)
    def _():
        copy(chunk(slot), me, slot, zs.at[0], zr.at[slot]).wait_recv()
        for j in range(1, 8):
            other = (slot + j) % 8

            @pl.when(other != 0)
            def _(other=other, j=j):
                copy(chunk(slot), me, other, zs.at[j], zr.at[slot]).start()

    first = row_at(x, y, core) * 1024 + slot * 128

    def count(i, total):
        lefts, rights = [], []
        for r in range(8):
            left, right = counts_step(jnp.broadcast_to(pairs_ref[pl.ds(i * 8 + r, 1), :], (8, 128))[0:1, :], first)
            lefts.append(left)
            rights.append(right)
        return total + dot_nt(jnp.concatenate(lefts, axis=1), jnp.concatenate(rights, axis=1))

    hits[:, 0:48] = lax.fori_loop(0, pairs_ref.shape[0] // 8, count, jnp.zeros((48, 48), F32))

    @pl.when(slot != 0)
    def _():
        for j in range(1, 8):
            other = (slot + j) % 8
            copy(chunk(other), me, slot, zs.at[0], zr.at[other]).wait_recv()

    near, far = pl.ds(0, 1024), pl.ds(1024, 1024)
    sent = []

    def send(view, row, i):
        c = copy(view, row, slot, ss.at[i], sr.at[i])
        c.start()
        sent.append(c)

    def arrive(view, i):
        copy(view, twin, slot, ss.at[i], sr.at[i]).wait_recv()

    passed = []

    def share(view, back, i):
        c = copy(view, twin, slot, cs.at[i], cr.at[i])
        c.start()
        passed.append((c, back, i))

    own_near, own_far = panel.at[x, y, core, :, near], panel.at[x, y, core, :, far]
    send(own_near, to_xp, 0)
    send(own_far, to_yp, 1)
    send(own_near, to_xm, 2)
    send(own_far, to_ym, 3)
    share(panel.at[x, y, core], panel.at[x, y, 1 - core], 0)
    top, low = pl.ds(0, 16), pl.ds(16, 16)
    arrive(panel.at[xm, y, core, :, near], 0)
    send(panel.at[xm, y, core, top, near], to_xp, 4)
    arrive(panel.at[x, ym, core, :, far], 1)
    send(panel.at[x, ym, core, top, far], to_yp, 5)
    arrive(panel.at[xp, y, core, :, near], 2)
    send(panel.at[xp, y, core, low, near], to_xm, 6)
    arrive(panel.at[x, yp, core, :, far], 3)
    send(panel.at[x, yp, core, low, far], to_ym, 7)
    share(panel.at[xm, y, core, :, near], panel.at[xm, y, 1 - core, :, near], 1)
    share(panel.at[x, ym, core, :, far], panel.at[x, ym, 1 - core, :, far], 2)
    share(panel.at[xp, y, core, :, near], panel.at[xp, y, 1 - core, :, near], 3)
    share(panel.at[x, yp, core, :, far], panel.at[x, yp, 1 - core, :, far], 4)
    arrive(panel.at[xo, y, core, top, near], 4)
    arrive(panel.at[xo, y, core, low, near], 6)
    send(panel.at[:, y, core, :, near], to_yp, 8)
    send(panel.at[:, y, core, :, near], to_ym, 10)
    arrive(panel.at[x, yo, core, top, far], 5)
    arrive(panel.at[x, yo, core, low, far], 7)
    send(panel.at[x, :, core, :, far], to_xp, 9)
    send(panel.at[x, :, core, :, far], to_xm, 11)
    share(panel.at[xo, y, core, :, near], panel.at[xo, y, 1 - core, :, near], 5)
    share(panel.at[x, yo, core, :, far], panel.at[x, yo, 1 - core, :, far], 6)

    row_hits = hits[:, 0:48]
    pextra_ref[...] = 0.1 + 0.5 * spread(row_hits[0:32, 0:32], 32)
    extra_ref[...] = 0.1 + 0.5 * spread(row_hits[32:40, 32:48], 16)

    first_two, last_two = pl.ds(0, 2), pl.ds(2, 2)
    arrive(panel.at[:, ym, core, :, near], 8)
    send(panel.at[first_two, ym, core, :, near], to_yp, 12)
    arrive(panel.at[xm, :, core, :, far], 9)
    send(panel.at[xm, first_two, core, :, far], to_xp, 13)
    arrive(panel.at[:, yp, core, :, near], 10)
    send(panel.at[last_two, yp, core, :, near], to_ym, 14)
    arrive(panel.at[xp, :, core, :, far], 11)
    send(panel.at[xp, last_two, core, :, far], to_xm, 15)
    share(panel.at[:, ym, core, :, near], panel.at[:, ym, 1 - core, :, near], 7)
    share(panel.at[xm, :, core, :, far], panel.at[xm, :, 1 - core, :, far], 8)
    share(panel.at[:, yp, core, :, near], panel.at[:, yp, 1 - core, :, near], 9)
    share(panel.at[xp, :, core, :, far], panel.at[xp, :, 1 - core, :, far], 10)
    arrive(panel.at[first_two, yo, core, :, near], 12)
    arrive(panel.at[last_two, yo, core, :, near], 14)
    share(panel.at[:, yo, core, :, near], panel.at[:, yo, 1 - core, :, near], 11)
    arrive(panel.at[xo, first_two, core, :, far], 13)
    arrive(panel.at[xo, last_two, core, :, far], 15)
    share(panel.at[xo, :, core, :, far], panel.at[xo, :, 1 - core, :, far], 12)
    for c, back, i in passed:
        copy(back, twin, slot, cs.at[i], cr.at[i]).wait_recv()
        c.wait_send()
    for c in sent:
        c.wait_send()

    @pl.when(slot == 0)
    def _():
        for c in range(1, 8):
            copy(chunk(c), me, c, zs.at[c], zr.at[c]).wait_send()
            copy(chunk(0), me, c, zs.at[7 + c], zr.at[0]).wait_send()

    @pl.when(slot != 0)
    def _():
        for j in range(1, 8):
            other = (slot + j) % 8

            @pl.when(other != 0)
            def _(other=other, j=j):
                copy(chunk(slot), me, other, zs.at[j], zr.at[slot]).wait_send()


def gather_panel(embeddings, inverse_scales, pairs):
    vmem = pl.BlockSpec(memory_space=pltpu.VMEM)
    return pl.pallas_call(
        gather_kernel,
        out_shape=(
            jax.ShapeDtypeStruct((LEAF, 2048), BF16),
            jax.ShapeDtypeStruct((SIDE, SIDE, 2, 32, 2048), BF16),
            jax.ShapeDtypeStruct((1, PANEL), F32),
            jax.ShapeDtypeStruct((1, LEAF), F32),
        ),
        in_specs=[vmem] * 3,
        out_specs=(vmem,) * 4,
        scratch_shapes=[
            pltpu.VMEM((48, 128), F32),
            pltpu.SemaphoreType.DMA((15,)),
            pltpu.SemaphoreType.DMA((8,)),
            pltpu.SemaphoreType.DMA((16,)),
            pltpu.SemaphoreType.DMA((16,)),
            pltpu.SemaphoreType.DMA((13,)),
            pltpu.SemaphoreType.DMA((13,)),
        ],
        compiler_params=pltpu.CompilerParams(
            collective_id=0, has_side_effects=True, vmem_limit_bytes=40 << 20
        ),
        name="panel_gather",
    )(embeddings, inverse_scales, pairs)


def to_lanes(column):
    return jnp.broadcast_to(column, (128, 128)).T[0:1, :]


def chain_steps(a, leaf, low, up):
    count = PANEL // LEAF
    r128 = lax.broadcasted_iota(jnp.int32, (LEAF, LEAF), 0)
    c128 = lax.broadcasted_iota(jnp.int32, (LEAF, LEAF), 1)
    lane = lax.broadcasted_iota(jnp.int32, (LEAF, PANEL), 1)

    def beside(x):
        high, lo = halves(x)
        return jnp.concatenate([high, high, lo], axis=1)

    def above(x):
        high, lo = halves(x)
        return jnp.concatenate([high, lo, high], axis=0)

    def inverse():
        w = jnp.where(r128 >= c128, leaf[...], 0.0)
        return w, w.T

    def block(k):
        return pl.ds(pl.multiple_of(k * LEAF, LEAF), LEAF)

    leaf_factor(a[0:LEAF, 0:LEAF], leaf)

    def step(m, unused):
        own, after = block(m), block(m + 1)
        w, wt = inverse()
        w3, t3 = beside(w), above(wt)
        next_low = dot(beside(a[after, own]), t3)
        next_up = dot(w3, above(a[own, after]))
        tile = a[after, after] - dot(beside(next_low), above(next_up))
        lcol = dot(beside(a[:, own]), t3)
        a[:, own] = lcol
        a[own, own] = wt
        low[...] = beside(lcol)
        low[own, :] = beside(wt)
        mine = a[own, :]
        later = lane >= (m + 1) * LEAF
        up[...] = above(jnp.where(later, dot(w3, above(mine)), 0.0))
        a[own, :] = jnp.where(later, 0.0, mine)
        for n in range(PANEL // 256):
            cols = slice(256 * n, 256 * n + 256)
            a[:, cols] = a[:, cols] - dot(low[...], up[:, cols])
        leaf_factor(tile, leaf)
        return unused

    lax.fori_loop(0, count - 1, step, 0)
    last = block(count - 1)
    w, wt = inverse()
    a[:, last] = dot(beside(a[:, last]), above(wt))
    a[last, last] = wt


def chain_kernel(panel_ref, extra_ref, xh_ref, xl_ref, sq_ref, a, leaf, low, up, sq_col):
    count = PANEL // LEAF
    for i in range(count):
        v = panel_ref[i * LEAF : (i + 1) * LEAF, :].astype(F32)
        s = jnp.sum(v * v, axis=1, keepdims=True)
        sq_col[i * LEAF : (i + 1) * LEAF, :] = jnp.broadcast_to(s, (LEAF, 128))
        sq_ref[0:1, i * LEAF : (i + 1) * LEAF] = to_lanes(s)
    row = lax.broadcasted_iota(jnp.int32, (PANEL, 256), 0)
    lane = lax.broadcasted_iota(jnp.int32, (PANEL, 256), 1)

    def build(n, unused):
        cols = pl.ds(pl.multiple_of(n * 256, 256), 256)
        g = dot_nt(panel_ref[...], panel_ref[cols, :])
        s = sq_col[...]
        k = jnp.exp(-0.5 * (jnp.concatenate([s, s], axis=1) + sq_ref[0:1, cols] - 2.0 * g))
        a[:, cols] = k + jnp.where(row == lane + n * 256, extra_ref[0:1, cols], 0.0)
        return unused

    lax.fori_loop(0, PANEL // 256, build, 0)
    chain_steps(a, leaf, low, up)

    def finish(k, unused):
        own = pl.ds(pl.multiple_of(k * LEAF, LEAF), LEAF)
        row = lax.broadcasted_iota(jnp.int32, (PANEL, LEAF), 0)
        value = jnp.where(row < (k + 1) * LEAF, a[:, own], 0.0)
        high, lo = halves(value)
        xh_ref[:, own] = high
        xl_ref[:, own] = lo
        return unused

    lax.fori_loop(0, count, finish, 0)


def chain(panel, extras):
    vmem = pl.BlockSpec(memory_space=pltpu.VMEM)
    return pl.pallas_call(
        chain_kernel,
        out_shape=(
            jax.ShapeDtypeStruct((PANEL, PANEL), BF16),
            jax.ShapeDtypeStruct((PANEL, PANEL), BF16),
            jax.ShapeDtypeStruct((1, PANEL), F32),
        ),
        in_specs=[vmem, vmem],
        out_specs=(vmem, vmem, vmem),
        scratch_shapes=[
            pltpu.VMEM((PANEL, PANEL), F32),
            pltpu.VMEM((LEAF, LEAF), F32),
            pltpu.VMEM((PANEL, 3 * LEAF), BF16),
            pltpu.VMEM((3 * LEAF, PANEL), BF16),
            pltpu.VMEM((PANEL, 128), F32),
        ],
        compiler_params=pltpu.CompilerParams(vmem_limit_bytes=60 << 20),
        cost_estimate=pl.CostEstimate(flops=100_000_000_000, bytes_accessed=10_000_000, transcendentals=0),
        name="panel_chain",
    )(panel, extras)


def trail_kernel(
    block_ref, own_ref, v1_ref, v2_ref, v3_ref, panel_ref, xh_ref, xl_ref, psq_ref, pextra_ref, extra_ref,
    trail_ref, factor_ref, rows, sq_col, sq_row, kh, kl, fh, fl, vh, vl,
):
    me = lax.axis_index("row")
    slot = lax.axis_index("col")
    row_count = lax.axis_size("row")
    total = 1024 + 3 * LEAF
    rows[0:1024, :] = block_ref[...]
    for s, ref in enumerate((v1_ref, v2_ref, v3_ref)):
        rows[1024 + s * LEAF : 1024 + (s + 1) * LEAF, :] = ref[...]

    def squares(i, unused):
        at = pl.ds(pl.multiple_of(i * LEAF, LEAF), LEAF)
        v = rows[at, :].astype(F32)
        s = jnp.sum(v * v, axis=1, keepdims=True)
        sq_col[at, :] = jnp.broadcast_to(s, (LEAF, 128))
        return unused

    lax.fori_loop(0, total // LEAF, squares, 0)
    own = pl.ds(pl.multiple_of(slot * LEAF, LEAF), LEAF)
    sq_row[0:1, 0:128] = sq_col[own, :].T[0:1, :]
    for s in range(3):
        sq_row[0:1, (s + 1) * LEAF : (s + 2) * LEAF] = sq_col[1024 + s * LEAF : 1024 + (s + 1) * LEAF, :].T[0:1, :]

    lead_row = lax.broadcasted_iota(jnp.int32, (32, 256), 0)
    lead_lane = lax.broadcasted_iota(jnp.int32, (32, 256), 1)

    def kernel_part(n, unused):
        cols = pl.ds(pl.multiple_of(n * 256, 256), 256)
        g = dot_nt(rows[...], panel_ref[cols, :])
        s = sq_col[...]
        k = jnp.exp(-0.5 * (jnp.concatenate([s, s], axis=1) + psq_ref[0:1, cols] - 2.0 * g))
        high, lo = halves(k)
        kh[:, cols] = high
        kl[:, cols] = lo
        extra = pextra_ref[0:1, cols]

        def fix(start, block, scale):
            part = k[start : start + 32, :]
            hit = lead_lane + n * 256 == block * 32 + lead_row
            part = part + jnp.where(hit, extra * scale, 0.0)
            high, lo = halves(part)
            kh[start : start + 32, cols] = high
            kl[start : start + 32, cols] = lo

        fix(0, me, 1.0)
        lead = jnp.where(slot == 0, 1.0, 0.0).astype(F32)
        for s in range(3):
            fix(1024 + s * LEAF, lax.rem(me + row_count - s - 1, row_count), lead)
        return unused

    lax.fori_loop(0, PANEL // 256, kernel_part, 0)
    for n in range(4):
        depth = 256 * (n + 1)
        cols = slice(256 * n, 256 * n + 256)
        f = dot(kh[:, :depth], xh_ref[:depth, cols])
        f = f + dot(kh[:, :depth], xl_ref[:depth, cols])
        f = f + dot(kl[:, :depth], xh_ref[:depth, cols])
        high, lo = halves(f)
        fh[:, cols] = high
        fl[:, cols] = lo
    factor_ref[...] = fh[own, :].astype(F32) + fl[own, :].astype(F32)
    vh[0:LEAF, :] = fh[own, :]
    vl[0:LEAF, :] = fl[own, :]
    vh[LEAF:, :] = fh[1024:, :]
    vl[LEAF:, :] = fl[1024:, :]
    r = lax.broadcasted_iota(jnp.int32, (256, LEAF), 0)
    c = lax.broadcasted_iota(jnp.int32, (256, LEAF), 1)

    def tile(i, unused):
        at = pl.ds(pl.multiple_of(i * 256, 256), 256)
        left = rows[at, :]
        g = jnp.concatenate([dot_nt(left, rows[own, :]), dot_nt(left, rows[1024:, :])], axis=1)
        s = sq_col[at, :]
        k = jnp.exp(-0.5 * (jnp.concatenate([s] * 4, axis=1) + sq_row[...] - 2.0 * g))
        ff = dot_nt(fh[at, :], vh[...])
        ff = ff + dot_nt(fh[at, :], vl[...])
        ff = ff + dot_nt(fl[at, :], vh[...])
        t = k - ff
        trail_ref[at, :] = t
        diagonal = jnp.where(r + i * 256 == c + slot * LEAF, extra_ref[0:1, :], 0.0)
        trail_ref[at, 0:LEAF] = t[:, 0:LEAF] + diagonal
        return unused

    lax.fori_loop(0, 4, tile, 0)


def trail(block, own, visitors, panel, xh, xl, psq, pextra, extra):
    vmem = pl.BlockSpec(memory_space=pltpu.VMEM)
    total = 1024 + 3 * LEAF
    return pl.pallas_call(
        trail_kernel,
        out_shape=(
            jax.ShapeDtypeStruct((1024, STOPS * LEAF), F32),
            jax.ShapeDtypeStruct((LEAF, PANEL), F32),
        ),
        in_specs=[vmem] * 11,
        out_specs=(vmem, vmem),
        scratch_shapes=[
            pltpu.VMEM((total, 2048), BF16),
            pltpu.VMEM((total, 128), F32),
            pltpu.VMEM((1, STOPS * LEAF), F32),
            pltpu.VMEM((total, PANEL), BF16),
            pltpu.VMEM((total, PANEL), BF16),
            pltpu.VMEM((total, PANEL), BF16),
            pltpu.VMEM((total, PANEL), BF16),
            pltpu.VMEM((STOPS * LEAF, PANEL), BF16),
            pltpu.VMEM((STOPS * LEAF, PANEL), BF16),
        ],
        compiler_params=pltpu.CompilerParams(vmem_limit_bytes=60 << 20),
        cost_estimate=pl.CostEstimate(flops=30_000_000_000, bytes_accessed=20_000_000, transcendentals=0),
        name="trailing",
    )(block, own, *visitors, panel, xh, xl, psq, pextra, extra)


def body(embeddings, inverse_scales, matches):
    row_count = lax.axis_size("row")
    pairs = matches.reshape(-1, 128, 2).transpose(0, 2, 1).reshape(-1, 128)
    scaled, panel, panel_extra, extra = gather_panel(embeddings, inverse_scales[None, :], pairs)
    panel = panel.reshape(PANEL, -1)
    early = (embeddings.astype(F32) * inverse_scales[None, :]).astype(BF16)
    block = lax.all_gather(early, "col", axis=0, tiled=True)
    visitors = [
        lax.ppermute(scaled, "row", [((i - s) % row_count, i) for i in range(row_count)])
        for s in range(1, STOPS)
    ]
    xh, xl, psq = chain(panel, panel_extra)
    return trail(block, scaled, visitors, panel, xh, xl, psq, panel_extra, extra)


def solution(mesh):
    return jax.shard_map(
        body,
        mesh=mesh,
        in_specs=(P(("row", "col"), None), P(), P()),
        out_specs=(P("row", "col"), P(("row", "col"), None)),
        check_vma=False,
    )
```

```python
import functools

import jax
import jax.numpy as jnp
from jax import lax
from jax.experimental import pallas as pl
from jax.experimental.pallas import tpu as pltpu
from jax.sharding import PartitionSpec as P

PANEL = 1024
STOPS = 4
LEAF = 128
AHEAD = 4
RING_THREE = 1
RING_FOUR = 5
F32 = jnp.float32
BF16 = jnp.bfloat16


def halves(x):
    high = x.astype(BF16)
    return high, (x - high.astype(F32)).astype(BF16)


def dot(a, b):
    return jnp.dot(a, b, preferred_element_type=F32)


def dot_nt(a, b):
    return lax.dot_general(a, b, (((1,), (1,)), ((), ())), preferred_element_type=F32)


def leaf_factor(tile, out_ref):
    n = LEAF
    groups = n // 8
    lane = lax.broadcasted_iota(jnp.int32, (8, 128), 1)
    rows = [tile[8 * i : 8 * i + 8, :] for i in range(groups)]

    def column(i, k):
        return jnp.broadcast_to(rows[i][:, k : k + 1], (8, 128))

    def one_row(x, r):
        return jnp.broadcast_to(x[r : r + 1, :], (8, 128))

    pending = [[column(i, k) for i in range(groups)] for k in range(AHEAD)]
    for k in range(n):
        g, r = divmod(k, 8)
        current = pending.pop(0)
        scale = lax.rsqrt(one_row(current[g], r))
        c = [current[i] * scale if i >= g else None for i in range(groups)]
        if k + AHEAD < n:
            pending.append([column(i, k + AHEAD) if i >= (k + AHEAD) // 8 else None for i in range(groups)])
        for j in range(len(pending)):
            gp, rp = divmod(k + 1 + j, 8)
            s = one_row(c[gp], rp)
            pending[j] = [pending[j][i] - c[i] * s if i >= gp else None for i in range(groups)]
        u = jnp.where(lane == k, scale, one_row(rows[g], r) * scale)
        out_ref[k : k + 1, :] = u[0:1, :]
        for i in range(g, groups):
            rows[i] = jnp.where(lane == k, 0.0, rows[i]) - c[i] * u


MESH = pl.DeviceIdType.MESH
SIDE = 4


def counts_step(values, first):
    sub32 = lax.broadcasted_iota(jnp.int32, (32, 128), 0)
    sub16 = lax.broadcasted_iota(jnp.int32, (16, 128), 0)
    place = jnp.where((values & 1023) < 32, values & 31, -1)
    inside = values - first
    part = jnp.where((inside >= 0) & (inside < 128), inside >> 4, -1)
    left = jnp.concatenate(
        [jnp.where(sub32 == values >> 10, 1.0, 0.0), jnp.where(sub16 == part, 1.0, 0.0)], axis=0
    ).astype(BF16)
    right = jnp.concatenate(
        [jnp.where(sub32 == place, 1.0, 0.0), jnp.where(sub16 == (values & 15), 1.0, 0.0)], axis=0
    ).astype(BF16)
    return left, right


def spread(table, width):
    n = table.shape[0]
    total = n * width
    tiled = jnp.concatenate([table] * n, axis=1)
    row = lax.broadcasted_iota(jnp.int32, (n, total), 0)
    lane = lax.broadcasted_iota(jnp.int32, (n, total), 1)
    return jnp.sum(jnp.where(lane >> (width.bit_length() - 1) == row, tiled, 0.0), axis=0, keepdims=True)


def to_lanes(column):
    return jnp.broadcast_to(column, (128, 128)).T[0:1, :]


def chain_steps(a, leaf, low, up, event):
    count = PANEL // LEAF
    r128 = lax.broadcasted_iota(jnp.int32, (LEAF, LEAF), 0)
    c128 = lax.broadcasted_iota(jnp.int32, (LEAF, LEAF), 1)
    lane = lax.broadcasted_iota(jnp.int32, (LEAF, PANEL), 1)

    def beside(x):
        high, lo = halves(x)
        return jnp.concatenate([high, high, lo], axis=1)

    def above(x):
        high, lo = halves(x)
        return jnp.concatenate([high, lo, high], axis=0)

    def inverse():
        w = jnp.where(r128 >= c128, leaf[...], 0.0)
        return w, w.T

    def block(k):
        return pl.ds(pl.multiple_of(k * LEAF, LEAF), LEAF)

    leaf_factor(a[0:LEAF, 0:LEAF], leaf)

    def step(m, unused):
        event(m)
        own, after = block(m), block(m + 1)
        w, wt = inverse()
        w3, t3 = beside(w), above(wt)
        next_low = dot(beside(a[after, own]), t3)
        next_up = dot(w3, above(a[own, after]))
        tile = a[after, after] - dot(beside(next_low), above(next_up))
        lcol = dot(beside(a[:, own]), t3)
        a[:, own] = lcol
        a[own, own] = wt
        low[...] = beside(lcol)
        low[own, :] = beside(wt)
        mine = a[own, :]
        later = lane >= (m + 1) * LEAF
        up[...] = above(jnp.where(later, dot(w3, above(mine)), 0.0))
        a[own, :] = jnp.where(later, 0.0, mine)
        for n in range(PANEL // 256):
            cols = slice(256 * n, 256 * n + 256)
            a[:, cols] = a[:, cols] - dot(low[...], up[:, cols])
        leaf_factor(tile, leaf)
        return unused

    lax.fori_loop(0, count - 1, step, 0)
    last = block(count - 1)
    w, wt = inverse()
    a[:, last] = dot(beside(a[:, last]), above(wt))
    a[last, last] = wt


def whole_kernel(
    emb_ref, inv_ref, pairs_ref, trail_ref, factor_ref,
    rows, panel, pextra, extra, hits, a, leaf, low, up, psq_col, psq_row, sq_col, sq_row,
    kh, kl, xh, xl, fh, fl, vh, vl, zs, zr, ss, sr, cs, cr, bs, br, vs, vr,
):
    me = lax.axis_index("row")
    slot = lax.axis_index("col")
    x, y, core = me // 8, (me // 2) % SIDE, me % 2
    xp, xm, xo = (x + 1) % SIDE, (x + 3) % SIDE, (x + 2) % SIDE
    yp, ym, yo = (y + 1) % SIDE, (y + 3) % SIDE, (y + 2) % SIDE

    def row_at(x, y, core):
        return (x * SIDE + y) * 2 + core

    to_xp, to_xm = row_at(xp, y, core), row_at(xm, y, core)
    to_yp, to_ym = row_at(x, yp, core), row_at(x, ym, core)
    twin = row_at(x, y, 1 - core)
    barrier = pltpu.get_barrier_semaphore()
    for other in (to_xp, to_xm, to_yp, to_ym, twin):
        pl.semaphore_signal(barrier, inc=1, device_id=(other, slot), device_id_type=MESH)
    for j in range(1, 8):
        pl.semaphore_signal(barrier, inc=1, device_id=(me, (slot + j) % 8), device_id_type=MESH)
    for j in range(1, STOPS):
        pl.semaphore_signal(barrier, inc=1, device_id=((me + j) % 32, slot), device_id_type=MESH)
        pl.semaphore_signal(barrier, inc=1, device_id=((me + 32 - j) % 32, slot), device_id_type=MESH)

    def scale(start, count):
        v = emb_ref[start : start + count, :].astype(F32) * inv_ref[0:1, :]
        rows[slot, start : start + count, :] = v.astype(BF16)

    scale(0, 32)

    @pl.when(slot == 0)
    def _():
        panel[x, y, core] = rows[slot, 0:32, :]

    pl.semaphore_wait(barrier, 12 + 2 * (STOPS - 1))

    def copy(view, row, col, send, recv):
        return pltpu.make_async_remote_copy(
            src_ref=view, dst_ref=view, send_sem=send, recv_sem=recv, device_id=(row, col), device_id_type=MESH
        )

    def chunk(q):
        return panel.at[x, y, core, :, pl.ds(pl.multiple_of(q * 256, 256), 256)]

    @pl.when(slot == 0)
    def _():
        for c in range(1, 8):
            copy(chunk(c), me, c, zs.at[c], zr.at[c]).start()
        for c in range(1, 8):
            copy(chunk(0), me, c, zs.at[7 + c], zr.at[0]).start()

    scale(32, 96)

    @pl.when(slot != 0)
    def _():
        copy(chunk(slot), me, slot, zs.at[0], zr.at[slot]).wait_recv()
        for j in range(1, 8):
            other = (slot + j) % 8

            @pl.when(other != 0)
            def _(other=other, j=j):
                copy(chunk(slot), me, other, zs.at[j], zr.at[slot]).start()

    first = row_at(x, y, core) * 1024 + slot * 128

    def count(i, total):
        lefts, rights = [], []
        for r in range(8):
            left, right = counts_step(jnp.broadcast_to(pairs_ref[pl.ds(i * 8 + r, 1), :], (8, 128))[0:1, :], first)
            lefts.append(left)
            rights.append(right)
        return total + dot_nt(jnp.concatenate(lefts, axis=1), jnp.concatenate(rights, axis=1))

    hits[:, 0:48] = lax.fori_loop(0, pairs_ref.shape[0] // 8, count, jnp.zeros((48, 48), F32))

    @pl.when(slot != 0)
    def _():
        for j in range(1, 8):
            other = (slot + j) % 8
            copy(chunk(other), me, slot, zs.at[0], zr.at[other]).wait_recv()

    upper, lower = pl.ds(0, 64), pl.ds(64, 64)

    def ring_views(h):
        up, down = (slot + 9 - h) % 8, (slot + 7 + h) % 8
        if h < 4:
            return rows.at[up], rows.at[down]
        return rows.at[up, upper], rows.at[down, lower]

    def arriving_views(h):
        up, down = (slot + 8 - h) % 8, (slot + h) % 8
        if h < 4:
            return rows.at[up], rows.at[down]
        return rows.at[up, upper], rows.at[down, lower]

    def ring_send(h):
        up, down = ring_views(h)
        copy(up, me, (slot + 1) % 8, bs.at[2 * h - 2], br.at[2 * h - 2]).start()
        copy(down, me, (slot + 7) % 8, bs.at[2 * h - 1], br.at[2 * h - 1]).start()

    def ring_arrive(h):
        up, down = arriving_views(h)
        copy(up, me, slot, bs.at[2 * h - 2], br.at[2 * h - 2]).wait_recv()
        copy(down, me, slot, bs.at[2 * h - 1], br.at[2 * h - 1]).wait_recv()

    def ring_sent(h):
        up, down = ring_views(h)
        copy(up, me, slot, bs.at[2 * h - 2], br.at[2 * h - 2]).wait_send()
        copy(down, me, slot, bs.at[2 * h - 1], br.at[2 * h - 1]).wait_send()

    def visit(j):
        return pltpu.make_async_remote_copy(
            src_ref=rows.at[slot], dst_ref=rows.at[7 + j], send_sem=vs.at[j - 1], recv_sem=vr.at[j - 1],
            device_id=((me + j) % 32, slot), device_id_type=MESH,
        )

    ring_send(1)
    near, far = pl.ds(0, 1024), pl.ds(1024, 1024)
    sent = []

    def send(view, row, i):
        c = copy(view, row, slot, ss.at[i], sr.at[i])
        c.start()
        sent.append(c)

    def arrive(view, i):
        copy(view, twin, slot, ss.at[i], sr.at[i]).wait_recv()

    passed = []

    def share(view, back, i):
        c = copy(view, twin, slot, cs.at[i], cr.at[i])
        c.start()
        passed.append((c, back, i))

    own_near, own_far = panel.at[x, y, core, :, near], panel.at[x, y, core, :, far]
    send(own_near, to_xp, 0)
    send(own_far, to_yp, 1)
    send(own_near, to_xm, 2)
    send(own_far, to_ym, 3)
    share(panel.at[x, y, core], panel.at[x, y, 1 - core], 0)
    top, bottom = pl.ds(0, 16), pl.ds(16, 16)
    arrive(panel.at[xm, y, core, :, near], 0)
    send(panel.at[xm, y, core, top, near], to_xp, 4)
    arrive(panel.at[x, ym, core, :, far], 1)
    send(panel.at[x, ym, core, top, far], to_yp, 5)
    arrive(panel.at[xp, y, core, :, near], 2)
    send(panel.at[xp, y, core, bottom, near], to_xm, 6)
    arrive(panel.at[x, yp, core, :, far], 3)
    send(panel.at[x, yp, core, bottom, far], to_ym, 7)
    share(panel.at[xm, y, core, :, near], panel.at[xm, y, 1 - core, :, near], 1)
    share(panel.at[x, ym, core, :, far], panel.at[x, ym, 1 - core, :, far], 2)
    share(panel.at[xp, y, core, :, near], panel.at[xp, y, 1 - core, :, near], 3)
    share(panel.at[x, yp, core, :, far], panel.at[x, yp, 1 - core, :, far], 4)
    arrive(panel.at[xo, y, core, top, near], 4)
    arrive(panel.at[xo, y, core, bottom, near], 6)
    send(panel.at[:, y, core, :, near], to_yp, 8)
    send(panel.at[:, y, core, :, near], to_ym, 10)
    arrive(panel.at[x, yo, core, top, far], 5)
    arrive(panel.at[x, yo, core, bottom, far], 7)
    send(panel.at[x, :, core, :, far], to_xp, 9)
    send(panel.at[x, :, core, :, far], to_xm, 11)
    share(panel.at[xo, y, core, :, near], panel.at[xo, y, 1 - core, :, near], 5)
    share(panel.at[x, yo, core, :, far], panel.at[x, yo, 1 - core, :, far], 6)

    ring_arrive(1)
    ring_send(2)
    row_hits = hits[:, 0:48]
    pextra[...] = 0.1 + 0.5 * spread(row_hits[0:32, 0:32], 32)
    extra[...] = 0.1 + 0.5 * spread(row_hits[32:40, 32:48], 16)

    first_two, last_two = pl.ds(0, 2), pl.ds(2, 2)
    arrive(panel.at[:, ym, core, :, near], 8)
    send(panel.at[first_two, ym, core, :, near], to_yp, 12)
    arrive(panel.at[xm, :, core, :, far], 9)
    send(panel.at[xm, first_two, core, :, far], to_xp, 13)
    arrive(panel.at[:, yp, core, :, near], 10)
    send(panel.at[last_two, yp, core, :, near], to_ym, 14)
    arrive(panel.at[xp, :, core, :, far], 11)
    send(panel.at[xp, last_two, core, :, far], to_xm, 15)
    share(panel.at[:, ym, core, :, near], panel.at[:, ym, 1 - core, :, near], 7)
    share(panel.at[xm, :, core, :, far], panel.at[xm, :, 1 - core, :, far], 8)
    share(panel.at[:, yp, core, :, near], panel.at[:, yp, 1 - core, :, near], 9)
    share(panel.at[xp, :, core, :, far], panel.at[xp, :, 1 - core, :, far], 10)
    arrive(panel.at[first_two, yo, core, :, near], 12)
    arrive(panel.at[last_two, yo, core, :, near], 14)
    share(panel.at[:, yo, core, :, near], panel.at[:, yo, 1 - core, :, near], 11)
    arrive(panel.at[xo, first_two, core, :, far], 13)
    arrive(panel.at[xo, last_two, core, :, far], 15)
    share(panel.at[xo, :, core, :, far], panel.at[xo, :, 1 - core, :, far], 12)
    for c, back, i in passed:
        copy(back, twin, slot, cs.at[i], cr.at[i]).wait_recv()
        c.wait_send()
    for j in range(1, STOPS):
        visit(j).start()

    def panel_rows(n):
        return panel[n].reshape(256, 2048)

    def panel_squares(n, unused):
        for q in range(2):
            v = panel_rows(n)[q * LEAF : (q + 1) * LEAF, :].astype(F32)
            s = jnp.sum(v * v, axis=1, keepdims=True)
            at = pl.ds(pl.multiple_of(n * 256 + q * LEAF, LEAF), LEAF)
            psq_col[at, :] = jnp.broadcast_to(s, (LEAF, 128))
            psq_row[0:1, at] = to_lanes(s)
        return unused

    lax.fori_loop(0, SIDE, panel_squares, 0)

    def build(n, unused):
        cols = pl.ds(pl.multiple_of(n * 256, 256), 256)
        g = dot_nt(panel[...].reshape(PANEL, 2048), panel_rows(n))
        s = psq_col[...]
        k = jnp.exp(-0.5 * (jnp.concatenate([s, s], axis=1) + psq_row[0:1, cols] - 2.0 * g))
        row = lax.broadcasted_iota(jnp.int32, (PANEL, 256), 0)
        lane = lax.broadcasted_iota(jnp.int32, (PANEL, 256), 1)
        a[:, cols] = k + jnp.where(row == lane + n * 256, pextra[0:1, cols], 0.0)
        return unused

    lax.fori_loop(0, SIDE, build, 0)

    def event(m):
        @pl.when(m == RING_THREE)
        def _():
            ring_arrive(2)
            ring_send(3)

        @pl.when(m == RING_FOUR)
        def _():
            ring_arrive(3)
            ring_send(4)

    chain_steps(a, leaf, low, up, event)

    def finish(k, unused):
        own = pl.ds(pl.multiple_of(k * LEAF, LEAF), LEAF)
        row = lax.broadcasted_iota(jnp.int32, (PANEL, LEAF), 0)
        value = jnp.where(row < (k + 1) * LEAF, a[:, own], 0.0)
        high, lo = halves(value)
        xh[:, own] = high
        xl[:, own] = lo
        return unused

    lax.fori_loop(0, PANEL // LEAF, finish, 0)
    ring_arrive(4)
    for j in range(1, STOPS):
        visit(j).wait_recv()
    total = 1024 + 3 * LEAF

    def all_rows():
        return rows[...].reshape(total, 2048)

    def squares(i, unused):
        v = rows[i].astype(F32)
        s = jnp.sum(v * v, axis=1, keepdims=True)
        sq_col[pl.ds(pl.multiple_of(i * LEAF, LEAF), LEAF), :] = jnp.broadcast_to(s, (LEAF, 128))
        return unused

    lax.fori_loop(0, total // LEAF, squares, 0)
    own = pl.ds(pl.multiple_of(slot * LEAF, LEAF), LEAF)
    sq_row[0:1, 0:128] = sq_col[own, :].T[0:1, :]
    for s in range(3):
        sq_row[0:1, (s + 1) * LEAF : (s + 2) * LEAF] = sq_col[1024 + s * LEAF : 1024 + (s + 1) * LEAF, :].T[0:1, :]
    lead_row = lax.broadcasted_iota(jnp.int32, (32, 256), 0)
    lead_lane = lax.broadcasted_iota(jnp.int32, (32, 256), 1)

    def kernel_part(n, unused):
        cols = pl.ds(pl.multiple_of(n * 256, 256), 256)
        g = dot_nt(all_rows(), panel_rows(n))
        s = sq_col[...]
        k = jnp.exp(-0.5 * (jnp.concatenate([s, s], axis=1) + psq_row[0:1, cols] - 2.0 * g))
        high, lo = halves(k)
        kh[:, cols] = high
        kl[:, cols] = lo
        more = pextra[0:1, cols]

        def fix(start, block, scale):
            part = k[start : start + 32, :]
            hit = lead_lane + n * 256 == block * 32 + lead_row
            part = part + jnp.where(hit, more * scale, 0.0)
            high, lo = halves(part)
            kh[start : start + 32, cols] = high
            kl[start : start + 32, cols] = lo

        fix(0, me, 1.0)
        lead = jnp.where(slot == 0, 1.0, 0.0).astype(F32)
        for s in range(3):
            fix(1024 + s * LEAF, (me + 31 - s) % 32, lead)
        return unused

    lax.fori_loop(0, SIDE, kernel_part, 0)
    for n in range(4):
        depth = 256 * (n + 1)
        cols = slice(256 * n, 256 * n + 256)
        f = dot(kh[:, :depth], xh[:depth, cols])
        f = f + dot(kh[:, :depth], xl[:depth, cols])
        f = f + dot(kl[:, :depth], xh[:depth, cols])
        high, lo = halves(f)
        fh[:, cols] = high
        fl[:, cols] = lo
    factor_ref[...] = fh[own, :].astype(F32) + fl[own, :].astype(F32)
    vh[0:LEAF, :] = fh[own, :]
    vl[0:LEAF, :] = fl[own, :]
    vh[LEAF:, :] = fh[1024:, :]
    vl[LEAF:, :] = fl[1024:, :]
    r = lax.broadcasted_iota(jnp.int32, (256, LEAF), 0)
    c = lax.broadcasted_iota(jnp.int32, (256, LEAF), 1)

    def tile(i, unused):
        at = pl.ds(pl.multiple_of(i * 256, 256), 256)
        left = rows[pl.ds(2 * i, 2)].reshape(256, 2048)
        g = jnp.concatenate([dot_nt(left, rows[slot]), dot_nt(left, rows[8:11].reshape(3 * LEAF, 2048))], axis=1)
        s = sq_col[at, :]
        k = jnp.exp(-0.5 * (jnp.concatenate([s] * 4, axis=1) + sq_row[...] - 2.0 * g))
        ff = dot_nt(fh[at, :], vh[...])
        ff = ff + dot_nt(fh[at, :], vl[...])
        ff = ff + dot_nt(fl[at, :], vh[...])
        t = k - ff
        trail_ref[at, :] = t
        diagonal = jnp.where(r + i * 256 == c + slot * LEAF, extra[0:1, :], 0.0)
        trail_ref[at, 0:LEAF] = t[:, 0:LEAF] + diagonal
        return unused

    lax.fori_loop(0, 4, tile, 0)
    for h in range(1, 5):
        ring_sent(h)
    for j in range(1, STOPS):
        visit(j).wait_send()
    for c in sent:
        c.wait_send()

    @pl.when(slot == 0)
    def _():
        for c in range(1, 8):
            copy(chunk(c), me, c, zs.at[c], zr.at[c]).wait_send()
            copy(chunk(0), me, c, zs.at[7 + c], zr.at[0]).wait_send()

    @pl.when(slot != 0)
    def _():
        for j in range(1, 8):
            other = (slot + j) % 8

            @pl.when(other != 0)
            def _(other=other, j=j):
                copy(chunk(slot), me, other, zs.at[j], zr.at[slot]).wait_send()


def whole(embeddings, inverse_scales, pairs):
    vmem = pl.BlockSpec(memory_space=pltpu.VMEM)
    total = 1024 + 3 * LEAF
    return pl.pallas_call(
        whole_kernel,
        out_shape=(
            jax.ShapeDtypeStruct((1024, STOPS * LEAF), F32),
            jax.ShapeDtypeStruct((LEAF, PANEL), F32),
        ),
        in_specs=[vmem] * 3,
        out_specs=(vmem, vmem),
        scratch_shapes=[
            pltpu.VMEM((11, LEAF, 2048), BF16),
            pltpu.VMEM((SIDE, SIDE, 2, 32, 2048), BF16),
            pltpu.VMEM((1, PANEL), F32),
            pltpu.VMEM((1, LEAF), F32),
            pltpu.VMEM((48, 128), F32),
            pltpu.VMEM((PANEL, PANEL), F32),
            pltpu.VMEM((LEAF, LEAF), F32),
            pltpu.VMEM((PANEL, 3 * LEAF), BF16),
            pltpu.VMEM((3 * LEAF, PANEL), BF16),
            pltpu.VMEM((PANEL, 128), F32),
            pltpu.VMEM((1, PANEL), F32),
            pltpu.VMEM((total, 128), F32),
            pltpu.VMEM((1, STOPS * LEAF), F32),
            pltpu.VMEM((total, PANEL), BF16),
            pltpu.VMEM((total, PANEL), BF16),
            pltpu.VMEM((PANEL, PANEL), BF16),
            pltpu.VMEM((PANEL, PANEL), BF16),
            pltpu.VMEM((total, PANEL), BF16),
            pltpu.VMEM((total, PANEL), BF16),
            pltpu.VMEM((STOPS * LEAF, PANEL), BF16),
            pltpu.VMEM((STOPS * LEAF, PANEL), BF16),
            pltpu.SemaphoreType.DMA((15,)),
            pltpu.SemaphoreType.DMA((8,)),
            pltpu.SemaphoreType.DMA((16,)),
            pltpu.SemaphoreType.DMA((16,)),
            pltpu.SemaphoreType.DMA((13,)),
            pltpu.SemaphoreType.DMA((13,)),
            pltpu.SemaphoreType.DMA((8,)),
            pltpu.SemaphoreType.DMA((8,)),
            pltpu.SemaphoreType.DMA((3,)),
            pltpu.SemaphoreType.DMA((3,)),
        ],
        compiler_params=pltpu.CompilerParams(
            collective_id=0, has_side_effects=True, vmem_limit_bytes=60 << 20
        ),
        name="whole",
    )(embeddings, inverse_scales, pairs)


def body(embeddings, inverse_scales, matches):
    pairs = matches.reshape(-1, 128, 2).transpose(0, 2, 1).reshape(-1, 128)
    return whole(embeddings, inverse_scales[None, :], pairs)


def solution(mesh):
    return jax.shard_map(
        body,
        mesh=mesh,
        in_specs=(P(("row", "col"), None), P(), P()),
        out_specs=(P("row", "col"), P(("row", "col"), None)),
        check_vma=False,
    )
```

```python
import functools

import jax
import jax.numpy as jnp
from jax import lax
from jax.experimental import pallas as pl
from jax.experimental.pallas import tpu as pltpu
from jax.sharding import PartitionSpec as P

PANEL = 1024
STOPS = 4
LEAF = 128
AHEAD = 4
F32 = jnp.float32
BF16 = jnp.bfloat16


def halves(x):
    high = x.astype(BF16)
    return high, (x - high.astype(F32)).astype(BF16)


def dot(a, b):
    return jnp.dot(a, b, preferred_element_type=F32)


def dot_nt(a, b):
    return lax.dot_general(a, b, (((1,), (1,)), ((), ())), preferred_element_type=F32)


def leaf_factor(tile, out_ref):
    n = LEAF
    groups = n // 8
    lane = lax.broadcasted_iota(jnp.int32, (8, 128), 1)
    rows = [tile[8 * i : 8 * i + 8, :] for i in range(groups)]

    def column(i, k):
        return jnp.broadcast_to(rows[i][:, k : k + 1], (8, 128))

    def one_row(x, r):
        return jnp.broadcast_to(x[r : r + 1, :], (8, 128))

    pending = [[column(i, k) for i in range(groups)] for k in range(AHEAD)]
    for k in range(n):
        g, r = divmod(k, 8)
        current = pending.pop(0)
        scale = lax.rsqrt(one_row(current[g], r))
        c = [current[i] * scale if i >= g else None for i in range(groups)]
        if k + AHEAD < n:
            pending.append([column(i, k + AHEAD) if i >= (k + AHEAD) // 8 else None for i in range(groups)])
        for j in range(len(pending)):
            gp, rp = divmod(k + 1 + j, 8)
            s = one_row(c[gp], rp)
            pending[j] = [pending[j][i] - c[i] * s if i >= gp else None for i in range(groups)]
        u = jnp.where(lane == k, scale, one_row(rows[g], r) * scale)
        out_ref[k : k + 1, :] = u[0:1, :]
        for i in range(g, groups):
            rows[i] = jnp.where(lane == k, 0.0, rows[i]) - c[i] * u


MESH = pl.DeviceIdType.MESH
SIDE = 4


def counts_step(values, first):
    sub32 = lax.broadcasted_iota(jnp.int32, (32, 128), 0)
    sub16 = lax.broadcasted_iota(jnp.int32, (16, 128), 0)
    block = values >> 10
    place = jnp.where((values & 1023) < 32, values & 31, -1)
    inside = values - first
    part = jnp.where((inside >= 0) & (inside < 128), inside >> 4, -1)
    unit = values & 15

    def marks(big, small, r):
        return jnp.concatenate(
            [
                jnp.where(sub32 == big[r : r + 1, :], 1.0, 0.0).astype(BF16),
                jnp.where(sub16 == small[r : r + 1, :], 1.0, 0.0).astype(BF16),
            ],
            axis=0,
        )

    return [marks(block, part, r) for r in range(8)], [marks(place, unit, r) for r in range(8)]


def spread(table, width):
    n = table.shape[0]
    total = n * width
    tiled = jnp.concatenate([table] * n, axis=1)
    row = lax.broadcasted_iota(jnp.int32, (n, total), 0)
    lane = lax.broadcasted_iota(jnp.int32, (n, total), 1)
    return jnp.sum(jnp.where(lane >> (width.bit_length() - 1) == row, tiled, 0.0), axis=0, keepdims=True)


def to_lanes(column):
    return jnp.broadcast_to(column, (128, 128)).T[0:1, :]


def chain_steps(a, leaf, low, up, xh, xl, event, one_slice, two_slices):
    count = PANEL // LEAF
    r128 = lax.broadcasted_iota(jnp.int32, (LEAF, LEAF), 0)
    c128 = lax.broadcasted_iota(jnp.int32, (LEAF, LEAF), 1)
    lane = lax.broadcasted_iota(jnp.int32, (LEAF, PANEL), 1)

    def beside(x):
        high, lo = halves(x)
        return jnp.concatenate([high, high, lo], axis=1)

    def above(x):
        high, lo = halves(x)
        return jnp.concatenate([high, lo, high], axis=0)

    def inverse():
        w = jnp.where(r128 >= c128, leaf[...], 0.0)
        return w, w.T

    def block(k):
        return pl.ds(pl.multiple_of(k * LEAF, LEAF), LEAF)

    def finish_column(m, lcol, wt):
        low[...] = beside(lcol)
        low[block(m), :] = beside(wt)
        row = lax.broadcasted_iota(jnp.int32, (PANEL, LEAF), 0)
        for half, out in ((slice(0, LEAF), xh), (slice(2 * LEAF, 3 * LEAF), xl)):
            out[:, block(m)] = jnp.where(row < (m + 1) * LEAF, low[:, half].astype(F32), 0.0).astype(BF16)

    leaf_factor(a[0:LEAF, 0:LEAF], leaf)

    def step(beside_leaf, m, unused):
        event(m)
        own, after = block(m), block(m + 1)
        w, wt = inverse()
        w3, t3 = beside(w), above(wt)
        next_low = dot(beside(a[after, own]), t3)
        next_up = dot(w3, above(a[own, after]))
        tile = a[after, after] - dot(beside(next_low), above(next_up))
        finish_column(m, dot(beside(a[:, own]), t3), wt)
        mine = a[own, :]
        later = lane >= (m + 1) * LEAF
        up[...] = above(jnp.where(later, dot(w3, above(mine)), 0.0))
        a[own, :] = jnp.where(later, 0.0, mine)
        for n in range(PANEL // 256):
            cols = slice(256 * n, 256 * n + 256)
            a[:, cols] = a[:, cols] - dot(low[...], up[:, cols])
        beside_leaf(m)
        leaf_factor(tile, leaf)
        return unused

    lax.fori_loop(0, 3, functools.partial(step, one_slice), 0)
    lax.fori_loop(3, count - 1, functools.partial(step, two_slices), 0)
    last = block(count - 1)
    w, wt = inverse()
    finish_column(count - 1, dot(beside(a[:, last]), above(wt)), wt)


def whole_kernel(
    emb_ref, inv_ref, pairs_ref, trail_ref, factor_ref,
    rows, panel, pextra, extra, hits, a, leaf, low, up, psq_col, psq_row, sq_col, sq_row,
    kh, kl, xh, xl, fh, fl, vh, vl, zs, zr, ss, sr, cs, cr, bs, br, vs, vr,
):
    me = lax.axis_index("row")
    slot = lax.axis_index("col")
    x, y, core = me // 8, (me // 2) % SIDE, me % 2
    xp, xm, xo = (x + 1) % SIDE, (x + 3) % SIDE, (x + 2) % SIDE
    yp, ym, yo = (y + 1) % SIDE, (y + 3) % SIDE, (y + 2) % SIDE

    def row_at(x, y, core):
        return (x * SIDE + y) * 2 + core

    to_xp, to_xm = row_at(xp, y, core), row_at(xm, y, core)
    to_yp, to_ym = row_at(x, yp, core), row_at(x, ym, core)
    twin = row_at(x, y, 1 - core)
    barrier = pltpu.get_barrier_semaphore()
    for other in (to_xp, to_xm, to_yp, to_ym, twin, row_at(xo, y, core), row_at(x, yo, core)):
        pl.semaphore_signal(barrier, inc=1, device_id=(other, slot), device_id_type=MESH)
    for j in range(1, 8):
        pl.semaphore_signal(barrier, inc=1, device_id=(me, (slot + j) % 8), device_id_type=MESH)
    for j in range(1, STOPS):
        pl.semaphore_signal(barrier, inc=1, device_id=((me + j) % 32, slot), device_id_type=MESH)
        pl.semaphore_signal(barrier, inc=1, device_id=((me + 32 - j) % 32, slot), device_id_type=MESH)

    def scale(start, count):
        v = emb_ref[start : start + count, :].astype(F32) * inv_ref[0:1, :]
        rows[slot, start : start + count, :] = v.astype(BF16)

    scale(0, 32)

    @pl.when(slot == 0)
    def _():
        panel[x, y, core] = rows[slot, 0:32, :]

    pl.semaphore_wait(barrier, 14 + 2 * (STOPS - 1))

    def copy(view, row, col, send, recv):
        return pltpu.make_async_remote_copy(
            src_ref=view, dst_ref=view, send_sem=send, recv_sem=recv, device_id=(row, col), device_id_type=MESH
        )

    def chunk(q):
        return panel.at[x, y, core, :, pl.ds(pl.multiple_of(q * 256, 256), 256)]

    @pl.when(slot == 0)
    def _():
        for c in range(1, 8):
            copy(chunk(c), me, c, zs.at[c], zr.at[c]).start()
        for c in range(1, 8):
            copy(chunk(0), me, c, zs.at[7 + c], zr.at[0]).start()

    scale(32, 96)

    @pl.when(slot != 0)
    def _():
        copy(chunk(slot), me, slot, zs.at[0], zr.at[slot]).wait_recv()
        for j in range(1, 8):
            other = (slot + j) % 8

            @pl.when(other != 0)
            def _(other=other, j=j):
                copy(chunk(slot), me, other, zs.at[j], zr.at[slot]).start()

    first = row_at(x, y, core) * 1024 + slot * 128

    def count(i, total):
        lefts, rights = [], []
        for q in range(4):
            left, right = counts_step(pairs_ref[pl.ds(pl.multiple_of(i * 32 + q * 8, 8), 8), :], first)
            lefts += left
            rights += right
        return total + dot_nt(jnp.concatenate(lefts, axis=1), jnp.concatenate(rights, axis=1))

    hits[:, 0:48] = lax.fori_loop(0, pairs_ref.shape[0] // 32, count, jnp.zeros((48, 48), F32))

    @pl.when(slot != 0)
    def _():
        for j in range(1, 8):
            other = (slot + j) % 8
            copy(chunk(other), me, slot, zs.at[0], zr.at[other]).wait_recv()

    upper, lower = pl.ds(0, 64), pl.ds(64, 64)

    def ring_views(h):
        up, down = (slot + 9 - h) % 8, (slot + 7 + h) % 8
        if h < 4:
            return rows.at[up], rows.at[down]
        return rows.at[up, upper], rows.at[down, lower]

    def arriving_views(h):
        up, down = (slot + 8 - h) % 8, (slot + h) % 8
        if h < 4:
            return rows.at[up], rows.at[down]
        return rows.at[up, upper], rows.at[down, lower]

    def ring_send(h):
        up, down = ring_views(h)
        copy(up, me, (slot + 1) % 8, bs.at[2 * h - 2], br.at[2 * h - 2]).start()
        copy(down, me, (slot + 7) % 8, bs.at[2 * h - 1], br.at[2 * h - 1]).start()

    def ring_arrive(h):
        up, down = arriving_views(h)
        copy(up, me, slot, bs.at[2 * h - 2], br.at[2 * h - 2]).wait_recv()
        copy(down, me, slot, bs.at[2 * h - 1], br.at[2 * h - 1]).wait_recv()

    def ring_sent(h):
        up, down = ring_views(h)
        copy(up, me, slot, bs.at[2 * h - 2], br.at[2 * h - 2]).wait_send()
        copy(down, me, slot, bs.at[2 * h - 1], br.at[2 * h - 1]).wait_send()

    def visitor_copy(src, dst, row, i):
        return pltpu.make_async_remote_copy(
            src_ref=rows.at[src], dst_ref=rows.at[dst], send_sem=vs.at[i], recv_sem=vr.at[i],
            device_id=(row, slot), device_id_type=MESH,
        )

    def visit_next():
        return visitor_copy(slot, 9, (me + 2) % 32, 0)

    def visit_relay():
        return visitor_copy(9, 10 - 2 * core, twin, 1)

    def visit_straight():
        return visitor_copy(slot, 8 + 2 * core, (me + 1 + 2 * core) % 32, 2)

    def visit_arrive(i, at):
        visitor_copy(at, at, twin, i).wait_recv()

    ring_send(1)
    near, far = pl.ds(0, 1024), pl.ds(1024, 1024)
    sent = []

    def send(view, row, i):
        c = copy(view, row, slot, ss.at[i], sr.at[i])
        c.start()
        sent.append(c)

    def arrive(view, i):
        copy(view, twin, slot, ss.at[i], sr.at[i]).wait_recv()

    passed = []

    def share(view, back, i):
        c = copy(view, twin, slot, cs.at[i], cr.at[i])
        c.start()
        passed.append((c, back, i))

    xs, ys = (x, xp, xo, xm), (y, yp, yo, ym)

    def piece(half, along, across):
        if half == 0:
            return panel.at[xs[along], ys[across], core, :, near]
        return panel.at[xs[across], ys[along], core, :, far]

    first_to = ((to_xp, to_xm), (to_yp, to_ym))
    far_to = (row_at(xo, y, core), row_at(x, yo, core))
    second_to = ((to_yp, to_ym), (to_xp, to_xm))

    def second(half, along):
        for way in range(2):
            send(piece(half, along, 0), second_to[half][way], 8 + half * 12 + along * 2 + way)

    def second_arrive(half, along, way):
        arrive(piece(half, along, 3 if way == 0 else 1), 8 + half * 12 + along * 2 + way)

    def second_pass(half, along, way):
        i = 16 + half * 12 + along
        send(piece(half, along, 3 if way == 0 else 1), second_to[half][way], i)

    for half in range(2):
        for way in range(2):
            send(piece(half, 0, 0), first_to[half][way], half * 4 + way)
    for half in range(2):
        send(piece(half, 0, 0), far_to[half], half * 4 + 2)
    for half in range(2):
        second(half, 0)
    share(panel.at[x, y, core], panel.at[x, y, 1 - core], 0)
    for half in range(2):
        arrive(piece(half, 3, 0), half * 4)
        arrive(piece(half, 1, 0), half * 4 + 1)
    for half in range(2):
        second(half, 3)
        second(half, 1)
    share(panel.at[xm, y, core, :, near], panel.at[xm, y, 1 - core, :, near], 1)
    share(panel.at[x, ym, core, :, far], panel.at[x, ym, 1 - core, :, far], 2)
    share(panel.at[xp, y, core, :, near], panel.at[xp, y, 1 - core, :, near], 3)
    share(panel.at[x, yp, core, :, far], panel.at[x, yp, 1 - core, :, far], 4)
    for half in range(2):
        second_arrive(half, 0, 0)
        second_pass(half, 0, 0)
    for half in range(2):
        arrive(piece(half, 2, 0), half * 4 + 2)
        second(half, 2)
    share(panel.at[xo, y, core, :, near], panel.at[xo, y, 1 - core, :, near], 5)
    share(panel.at[x, yo, core, :, far], panel.at[x, yo, 1 - core, :, far], 6)
    for half in range(2):
        second_arrive(half, 0, 1)
        second_arrive(half, 3, 1)
        second_pass(half, 3, 1)
        second_arrive(half, 1, 0)
        second_pass(half, 1, 0)

    row_hits = hits[:, 0:48]
    pextra[...] = 0.1 + 0.5 * spread(row_hits[0:32, 0:32], 32)
    extra[...] = 0.1 + 0.5 * spread(row_hits[32:40, 32:48], 16)

    for half in range(2):
        second_arrive(half, 3, 0)
        second_arrive(half, 1, 1)
    for half in range(2):
        second_arrive(half, 2, 1)
        second_pass(half, 2, 1)
        second_arrive(half, 2, 0)
    share(panel.at[:, ym, core, :, near], panel.at[:, ym, 1 - core, :, near], 7)
    share(panel.at[xm, :, core, :, far], panel.at[xm, :, 1 - core, :, far], 8)
    share(panel.at[:, yp, core, :, near], panel.at[:, yp, 1 - core, :, near], 9)
    share(panel.at[xp, :, core, :, far], panel.at[xp, :, 1 - core, :, far], 10)
    ring_arrive(1)
    ring_send(2)
    for half in range(2):
        for along in range(4):
            arrive(piece(half, along, 2), 16 + half * 12 + along)
    share(panel.at[:, yo, core, :, near], panel.at[:, yo, 1 - core, :, near], 11)
    share(panel.at[xo, :, core, :, far], panel.at[xo, :, 1 - core, :, far], 12)
    for c, back, i in passed:
        copy(back, twin, slot, cs.at[i], cr.at[i]).wait_recv()
        c.wait_send()
    visit_next().start()

    def panel_rows(n):
        return panel[n].reshape(256, 2048)

    def panel_squares(n, unused):
        for q in range(2):
            v = panel_rows(n)[q * LEAF : (q + 1) * LEAF, :].astype(F32)
            s = jnp.sum(v * v, axis=1, keepdims=True)
            at = pl.ds(pl.multiple_of(n * 256 + q * LEAF, LEAF), LEAF)
            psq_col[at, :] = jnp.broadcast_to(s, (LEAF, 128))
            psq_row[0:1, at] = to_lanes(s)
        return unused

    lax.fori_loop(0, SIDE, panel_squares, 0)

    def build(n, unused):
        cols = pl.ds(pl.multiple_of(n * 256, 256), 256)
        g = dot_nt(panel[...].reshape(PANEL, 2048), panel_rows(n))
        s = psq_col[...]
        k = jnp.exp(-0.5 * (jnp.concatenate([s, s], axis=1) + psq_row[0:1, cols] - 2.0 * g))
        row = lax.broadcasted_iota(jnp.int32, (PANEL, 256), 0)
        lane = lax.broadcasted_iota(jnp.int32, (PANEL, 256), 1)
        a[:, cols] = k + jnp.where(row == lane + n * 256, pextra[0:1, cols], 0.0)
        return unused

    lax.fori_loop(0, SIDE, build, 0)

    def event(m):
        @pl.when(m == 1)
        def _():
            ring_arrive(2)
            ring_send(3)
            visit_arrive(0, 9)
            visit_relay().start()
            visit_straight().start()

        @pl.when(m == 4)
        def _():
            ring_arrive(3)
            ring_send(4)

        @pl.when(m == 5)
        def _():
            visit_arrive(1, 8 + 2 * core)
            visit_arrive(2, 10 - 2 * core)

        @pl.when(m == 6)
        def _():
            ring_arrive(4)

    lead_row = lax.broadcasted_iota(jnp.int32, (32, PANEL), 0)
    lead_lane = lax.broadcasted_iota(jnp.int32, (32, PANEL), 1)

    def kernel_rows(slices):
        parts = []
        for i, block_id, leads in slices:
            v = rows[i].astype(F32)
            parts.append(jnp.sum(v * v, axis=1, keepdims=True))
            sq_col[pl.ds(pl.multiple_of(i * LEAF, LEAF), LEAF), :] = jnp.broadcast_to(parts[-1], (LEAF, 128))
        left = jnp.concatenate([rows[i] for i, block_id, leads in slices], axis=0)
        g = dot_nt(left, panel[...].reshape(PANEL, 2048))
        k = jnp.exp(-0.5 * (jnp.concatenate(parts, axis=0) + psq_row[0:1, :] - 2.0 * g))
        for q, (i, block_id, leads) in enumerate(slices):
            hit = lead_lane == block_id * 32 + lead_row
            top_rows = k[q * LEAF : q * LEAF + 32, :] + jnp.where(hit, pextra[0:1, :] * leads, 0.0)
            high, lo = halves(jnp.concatenate([top_rows, k[q * LEAF + 32 : (q + 1) * LEAF, :]], axis=0))
            at = pl.ds(pl.multiple_of(i * LEAF, LEAF), LEAF)
            kh[at, :] = high
            kl[at, :] = lo

    def is_zero(i):
        return jnp.where(i == 0, 1.0, 0.0).astype(F32)

    def one_slice(m):
        away = (m + 1) // 2
        i = (slot + 8 + away - 2 * away * (m % 2)) % 8
        kernel_rows([(i, me, is_zero(i))])

    def two_slices(m):
        late, last = m // 5, m // 6
        early = 1 - late
        i = early * ((slot + 9 - m) % 8) + late * (4 + m)
        i_block = early * me + late * ((me + 35 - m) % 32)
        j = early * ((slot + m - 1) % 8) + (late - last) * 8 + last * ((slot + 4) % 8)
        j_block = (1 - late + last) * me + (late - last) * ((me + 31) % 32)
        i_slice = early * i + late * slot
        j_slice = (1 - late + last) * j + (late - last) * slot
        kernel_rows([(i, i_block, is_zero(i_slice)), (j, j_block, is_zero(j_slice))])

    chain_steps(a, leaf, low, up, xh, xl, event, one_slice, two_slices)
    own = pl.ds(pl.multiple_of(slot * LEAF, LEAF), LEAF)
    sq_row[0:1, 0:128] = sq_col[own, :].T[0:1, :]
    for s in range(3):
        sq_row[0:1, (s + 1) * LEAF : (s + 2) * LEAF] = sq_col[1024 + s * LEAF : 1024 + (s + 1) * LEAF, :].T[0:1, :]
    for n in range(4):
        depth = 256 * (n + 1)
        cols = slice(256 * n, 256 * n + 256)
        f = dot(kh[:, :depth], xh[:depth, cols])
        f = f + dot(kh[:, :depth], xl[:depth, cols])
        f = f + dot(kl[:, :depth], xh[:depth, cols])
        high, lo = halves(f)
        fh[:, cols] = high
        fl[:, cols] = lo
    factor_ref[...] = fh[own, :].astype(F32) + fl[own, :].astype(F32)
    vh[0:LEAF, :] = fh[own, :]
    vl[0:LEAF, :] = fl[own, :]
    vh[LEAF:, :] = fh[1024:, :]
    vl[LEAF:, :] = fl[1024:, :]
    r = lax.broadcasted_iota(jnp.int32, (256, LEAF), 0)
    c = lax.broadcasted_iota(jnp.int32, (256, LEAF), 1)

    def tile(i, unused):
        at = pl.ds(pl.multiple_of(i * 256, 256), 256)
        left = rows[pl.ds(2 * i, 2)].reshape(256, 2048)
        g = jnp.concatenate([dot_nt(left, rows[slot]), dot_nt(left, rows[8:11].reshape(3 * LEAF, 2048))], axis=1)
        s = sq_col[at, :]
        k = jnp.exp(-0.5 * (jnp.concatenate([s] * 4, axis=1) + sq_row[...] - 2.0 * g))
        ff = dot_nt(fh[at, :], vh[...])
        ff = ff + dot_nt(fh[at, :], vl[...])
        ff = ff + dot_nt(fl[at, :], vh[...])
        t = k - ff
        trail_ref[at, :] = t
        diagonal = jnp.where(r + i * 256 == c + slot * LEAF, extra[0:1, :], 0.0)
        trail_ref[at, 0:LEAF] = t[:, 0:LEAF] + diagonal
        return unused

    lax.fori_loop(0, 4, tile, 0)
    for h in range(1, 5):
        ring_sent(h)
    visit_next().wait_send()
    visit_relay().wait_send()
    visit_straight().wait_send()
    for c in sent:
        c.wait_send()

    @pl.when(slot == 0)
    def _():
        for c in range(1, 8):
            copy(chunk(c), me, c, zs.at[c], zr.at[c]).wait_send()
            copy(chunk(0), me, c, zs.at[7 + c], zr.at[0]).wait_send()

    @pl.when(slot != 0)
    def _():
        for j in range(1, 8):
            other = (slot + j) % 8

            @pl.when(other != 0)
            def _(other=other, j=j):
                copy(chunk(slot), me, other, zs.at[j], zr.at[slot]).wait_send()


def whole(embeddings, inverse_scales, pairs):
    vmem = pl.BlockSpec(memory_space=pltpu.VMEM)
    total = 1024 + 3 * LEAF
    return pl.pallas_call(
        whole_kernel,
        out_shape=(
            jax.ShapeDtypeStruct((1024, STOPS * LEAF), F32),
            jax.ShapeDtypeStruct((LEAF, PANEL), F32),
        ),
        in_specs=[vmem] * 3,
        out_specs=(vmem, vmem),
        scratch_shapes=[
            pltpu.VMEM((11, LEAF, 2048), BF16),
            pltpu.VMEM((SIDE, SIDE, 2, 32, 2048), BF16),
            pltpu.VMEM((1, PANEL), F32),
            pltpu.VMEM((1, LEAF), F32),
            pltpu.VMEM((48, 128), F32),
            pltpu.VMEM((PANEL, PANEL), F32),
            pltpu.VMEM((LEAF, LEAF), F32),
            pltpu.VMEM((PANEL, 3 * LEAF), BF16),
            pltpu.VMEM((3 * LEAF, PANEL), BF16),
            pltpu.VMEM((PANEL, 128), F32),
            pltpu.VMEM((1, PANEL), F32),
            pltpu.VMEM((total, 128), F32),
            pltpu.VMEM((1, STOPS * LEAF), F32),
            pltpu.VMEM((total, PANEL), BF16),
            pltpu.VMEM((total, PANEL), BF16),
            pltpu.VMEM((PANEL, PANEL), BF16),
            pltpu.VMEM((PANEL, PANEL), BF16),
            pltpu.VMEM((total, PANEL), BF16),
            pltpu.VMEM((total, PANEL), BF16),
            pltpu.VMEM((STOPS * LEAF, PANEL), BF16),
            pltpu.VMEM((STOPS * LEAF, PANEL), BF16),
            pltpu.SemaphoreType.DMA((15,)),
            pltpu.SemaphoreType.DMA((8,)),
            pltpu.SemaphoreType.DMA((32,)),
            pltpu.SemaphoreType.DMA((32,)),
            pltpu.SemaphoreType.DMA((13,)),
            pltpu.SemaphoreType.DMA((13,)),
            pltpu.SemaphoreType.DMA((8,)),
            pltpu.SemaphoreType.DMA((8,)),
            pltpu.SemaphoreType.DMA((3,)),
            pltpu.SemaphoreType.DMA((3,)),
        ],
        compiler_params=pltpu.CompilerParams(
            collective_id=0, has_side_effects=True, vmem_limit_bytes=44 << 20
        ),
        name="whole",
    )(embeddings, inverse_scales, pairs)


def body(embeddings, inverse_scales, matches):
    pairs = matches.reshape(-1, 128, 2).transpose(0, 2, 1).reshape(-1, 128)
    return whole(embeddings, inverse_scales[None, :], pairs)


def solution(mesh):
    return jax.shard_map(
        body,
        mesh=mesh,
        in_specs=(P(("row", "col"), None), P(), P()),
        out_specs=(P("row", "col"), P(("row", "col"), None)),
        check_vma=False,
    )
```

```python
import functools

import jax
import jax.numpy as jnp
from jax import lax
from jax.experimental import pallas as pl
from jax.experimental.pallas import tpu as pltpu
from jax.sharding import PartitionSpec as P

PANEL = 1024
STOPS = 4
LEAF = 128
AHEAD = 4
F32 = jnp.float32
BF16 = jnp.bfloat16


def halves(x):
    high = x.astype(BF16)
    return high, (x - high.astype(F32)).astype(BF16)


def dot(a, b):
    return jnp.dot(a, b, preferred_element_type=F32)


def dot_nt(a, b):
    return lax.dot_general(a, b, (((1,), (1,)), ((), ())), preferred_element_type=F32)


def leaf_factor(tile, out_ref):
    n = LEAF
    groups = n // 8
    lane = lax.broadcasted_iota(jnp.int32, (8, 128), 1)
    rows = [tile[8 * i : 8 * i + 8, :] for i in range(groups)]

    def column(i, k):
        return jnp.broadcast_to(rows[i][:, k : k + 1], (8, 128))

    def one_row(x, r):
        return jnp.broadcast_to(x[r : r + 1, :], (8, 128))

    pending = [[column(i, k) for i in range(groups)] for k in range(AHEAD)]
    for k in range(n):
        g, r = divmod(k, 8)
        current = pending.pop(0)
        scale = lax.rsqrt(one_row(current[g], r))
        c = [current[i] * scale if i >= g else None for i in range(groups)]
        if k + AHEAD < n:
            pending.append([column(i, k + AHEAD) if i >= (k + AHEAD) // 8 else None for i in range(groups)])
        for j in range(len(pending)):
            gp, rp = divmod(k + 1 + j, 8)
            s = one_row(c[gp], rp)
            pending[j] = [pending[j][i] - c[i] * s if i >= gp else None for i in range(groups)]
        u = jnp.where(lane == k, scale, one_row(rows[g], r) * scale)
        out_ref[k : k + 1, :] = u[0:1, :]
        for i in range(g, groups):
            rows[i] = jnp.where(lane == k, 0.0, rows[i]) - c[i] * u


MESH = pl.DeviceIdType.MESH
SIDE = 4


def counts_step(values, first):
    sub32 = lax.broadcasted_iota(jnp.int32, (32, 128), 0)
    sub16 = lax.broadcasted_iota(jnp.int32, (16, 128), 0)
    block = values >> 10
    place = jnp.where((values & 1023) < 32, values & 31, -1)
    inside = values - first
    part = jnp.where((inside >= 0) & (inside < 128), inside >> 4, -1)
    unit = values & 15

    def marks(big, small, r):
        return jnp.concatenate(
            [
                jnp.where(sub32 == big[r : r + 1, :], 1.0, 0.0).astype(BF16),
                jnp.where(sub16 == small[r : r + 1, :], 1.0, 0.0).astype(BF16),
            ],
            axis=0,
        )

    return [marks(block, part, r) for r in range(8)], [marks(place, unit, r) for r in range(8)]


def spread(table, width):
    n = table.shape[0]
    total = n * width
    tiled = jnp.concatenate([table] * n, axis=1)
    row = lax.broadcasted_iota(jnp.int32, (n, total), 0)
    lane = lax.broadcasted_iota(jnp.int32, (n, total), 1)
    return jnp.sum(jnp.where(lane >> (width.bit_length() - 1) == row, tiled, 0.0), axis=0, keepdims=True)


def to_lanes(column):
    return jnp.broadcast_to(column, (128, 128)).T[0:1, :]


def chain_steps(a, leaf, low, up, xh, xl, event, one_slice, two_slices):
    count = PANEL // LEAF
    r128 = lax.broadcasted_iota(jnp.int32, (LEAF, LEAF), 0)
    c128 = lax.broadcasted_iota(jnp.int32, (LEAF, LEAF), 1)
    lane = lax.broadcasted_iota(jnp.int32, (LEAF, PANEL), 1)

    def beside(x):
        high, lo = halves(x)
        return jnp.concatenate([high, high, lo], axis=1)

    def above(x):
        high, lo = halves(x)
        return jnp.concatenate([high, lo, high], axis=0)

    def inverse():
        w = jnp.where(r128 >= c128, leaf[...], 0.0)
        return w, w.T

    def block(k):
        return pl.ds(pl.multiple_of(k * LEAF, LEAF), LEAF)

    def finish_column(m, lcol, wt):
        low[...] = beside(lcol)
        low[block(m), :] = beside(wt)
        row = lax.broadcasted_iota(jnp.int32, (PANEL, LEAF), 0)
        for half, out in ((slice(0, LEAF), xh), (slice(2 * LEAF, 3 * LEAF), xl)):
            out[:, block(m)] = jnp.where(row < (m + 1) * LEAF, low[:, half].astype(F32), 0.0).astype(BF16)

    leaf_factor(a[0:LEAF, 0:LEAF], leaf)

    def step(beside_leaf, m, unused):
        event(m)
        own, after = block(m), block(m + 1)
        w, wt = inverse()
        w3, t3 = beside(w), above(wt)
        next_low = dot(beside(a[after, own]), t3)
        next_up = dot(w3, above(a[own, after]))
        tile = a[after, after] - dot(beside(next_low), above(next_up))
        finish_column(m, dot(beside(a[:, own]), t3), wt)
        mine = a[own, :]
        later = lane >= (m + 1) * LEAF
        up[...] = above(jnp.where(later, dot(w3, above(mine)), 0.0))
        a[own, :] = jnp.where(later, 0.0, mine)
        for n in range(PANEL // 256):
            cols = slice(256 * n, 256 * n + 256)
            a[:, cols] = a[:, cols] - dot(low[...], up[:, cols])
        beside_leaf(m)
        leaf_factor(tile, leaf)
        return unused

    lax.fori_loop(0, 3, functools.partial(step, one_slice), 0)
    lax.fori_loop(3, count - 1, functools.partial(step, two_slices), 0)
    last = block(count - 1)
    w, wt = inverse()
    finish_column(count - 1, dot(beside(a[:, last]), above(wt)), wt)


def whole_kernel(
    emb_ref, inv_ref, pairs_ref, trail_ref, factor_ref,
    rows, panel, pextra, extra, hits, a, leaf, low, up, psq_col, psq_row, sq_col, sq_row,
    kh, kl, xh, xl, fh, fl, vh, vl, zs, zr, ss, sr, cs, cr, bs, br, vs, vr,
):
    me = lax.axis_index("row")
    slot = lax.axis_index("col")
    x, y, core = me // 8, (me // 2) % SIDE, me % 2
    xp, xm, xo = (x + 1) % SIDE, (x + 3) % SIDE, (x + 2) % SIDE
    yp, ym, yo = (y + 1) % SIDE, (y + 3) % SIDE, (y + 2) % SIDE

    def row_at(x, y, core):
        return (x * SIDE + y) * 2 + core

    to_xp, to_xm = row_at(xp, y, core), row_at(xm, y, core)
    to_yp, to_ym = row_at(x, yp, core), row_at(x, ym, core)
    twin = row_at(x, y, 1 - core)
    barrier = pltpu.get_barrier_semaphore()
    for other in (to_xp, to_xm, to_yp, to_ym, twin, row_at(xo, y, core), row_at(x, yo, core)):
        pl.semaphore_signal(barrier, inc=1, device_id=(other, slot), device_id_type=MESH)
    for j in range(1, 8):
        pl.semaphore_signal(barrier, inc=1, device_id=(me, (slot + j) % 8), device_id_type=MESH)
    for j in range(1, STOPS):
        pl.semaphore_signal(barrier, inc=1, device_id=((me + j) % 32, slot), device_id_type=MESH)
        pl.semaphore_signal(barrier, inc=1, device_id=((me + 32 - j) % 32, slot), device_id_type=MESH)

    def scale(start, count):
        v = emb_ref[start : start + count, :].astype(F32) * inv_ref[0:1, :]
        rows[slot, start : start + count, :] = v.astype(BF16)

    scale(0, 32)

    @pl.when(slot == 0)
    def _():
        panel[x, y, core] = rows[slot, 0:32, :]

    pl.semaphore_wait(barrier, 14 + 2 * (STOPS - 1))

    def copy(view, row, col, send, recv):
        return pltpu.make_async_remote_copy(
            src_ref=view, dst_ref=view, send_sem=send, recv_sem=recv, device_id=(row, col), device_id_type=MESH
        )

    def chunk(q):
        return panel.at[x, y, core, :, pl.ds(pl.multiple_of(q * 256, 256), 256)]

    @pl.when(slot == 0)
    def _():
        for c in range(1, 8):
            copy(chunk(c), me, c, zs.at[c], zr.at[c]).start()
        for c in range(1, 8):
            copy(chunk(0), me, c, zs.at[7 + c], zr.at[0]).start()

    scale(32, 96)

    @pl.when(slot != 0)
    def _():
        copy(chunk(slot), me, slot, zs.at[0], zr.at[slot]).wait_recv()
        for j in range(1, 8):
            other = (slot + j) % 8

            @pl.when(other != 0)
            def _(other=other, j=j):
                copy(chunk(slot), me, other, zs.at[j], zr.at[slot]).start()

    first = row_at(x, y, core) * 1024 + slot * 128

    def count(i, total):
        lefts, rights = [], []
        for q in range(4):
            left, right = counts_step(pairs_ref[pl.ds(pl.multiple_of(i * 32 + q * 8, 8), 8), :], first)
            lefts += left
            rights += right
        return total + dot_nt(jnp.concatenate(lefts, axis=1), jnp.concatenate(rights, axis=1))

    hits[:, 0:48] = lax.fori_loop(0, pairs_ref.shape[0] // 32, count, jnp.zeros((48, 48), F32))

    @pl.when(slot != 0)
    def _():
        for j in range(1, 8):
            other = (slot + j) % 8
            copy(chunk(other), me, slot, zs.at[0], zr.at[other]).wait_recv()

    upper, lower = pl.ds(0, 64), pl.ds(64, 64)

    def ring_views(h):
        up, down = (slot + 9 - h) % 8, (slot + 7 + h) % 8
        if h < 4:
            return rows.at[up], rows.at[down]
        return rows.at[up, upper], rows.at[down, lower]

    def arriving_views(h):
        up, down = (slot + 8 - h) % 8, (slot + h) % 8
        if h < 4:
            return rows.at[up], rows.at[down]
        return rows.at[up, upper], rows.at[down, lower]

    def ring_send(h):
        up, down = ring_views(h)
        copy(up, me, (slot + 1) % 8, bs.at[2 * h - 2], br.at[2 * h - 2]).start()
        copy(down, me, (slot + 7) % 8, bs.at[2 * h - 1], br.at[2 * h - 1]).start()

    def ring_arrive(h):
        up, down = arriving_views(h)
        copy(up, me, slot, bs.at[2 * h - 2], br.at[2 * h - 2]).wait_recv()
        copy(down, me, slot, bs.at[2 * h - 1], br.at[2 * h - 1]).wait_recv()

    def ring_sent(h):
        up, down = ring_views(h)
        copy(up, me, slot, bs.at[2 * h - 2], br.at[2 * h - 2]).wait_send()
        copy(down, me, slot, bs.at[2 * h - 1], br.at[2 * h - 1]).wait_send()

    def visitor_copy(src, dst, row, i):
        return pltpu.make_async_remote_copy(
            src_ref=rows.at[src], dst_ref=rows.at[dst], send_sem=vs.at[i], recv_sem=vr.at[i],
            device_id=(row, slot), device_id_type=MESH,
        )

    def visit_next():
        return visitor_copy(slot, 9, (me + 2) % 32, 0)

    def visit_relay():
        return visitor_copy(9, 10 - 2 * core, twin, 1)

    def visit_straight():
        return visitor_copy(slot, 8 + 2 * core, (me + 1 + 2 * core) % 32, 2)

    def visit_arrive(i, at):
        visitor_copy(at, at, twin, i).wait_recv()

    ring_send(1)
    near, far = pl.ds(0, 1024), pl.ds(1024, 1024)
    sent = []

    def send(view, row, i):
        c = copy(view, row, slot, ss.at[i], sr.at[i])
        c.start()
        sent.append(c)

    def arrive(view, i):
        copy(view, twin, slot, ss.at[i], sr.at[i]).wait_recv()

    passed = []

    def share(view, back, i):
        c = copy(view, twin, slot, cs.at[i], cr.at[i])
        c.start()
        passed.append((c, back, i))

    xs, ys = (x, xp, xo, xm), (y, yp, yo, ym)

    def piece(half, along, across):
        if half == 0:
            return panel.at[xs[along], ys[across], core, :, near]
        return panel.at[xs[across], ys[along], core, :, far]

    first_to = ((to_xp, to_xm), (to_yp, to_ym))
    far_to = (row_at(xo, y, core), row_at(x, yo, core))
    second_to = ((to_yp, to_ym), (to_xp, to_xm))

    def second(half, along):
        for way in range(2):
            send(piece(half, along, 0), second_to[half][way], 8 + half * 12 + along * 2 + way)

    def second_arrive(half, along, way):
        arrive(piece(half, along, 3 if way == 0 else 1), 8 + half * 12 + along * 2 + way)

    def second_pass(half, along, way):
        i = 16 + half * 12 + along
        send(piece(half, along, 3 if way == 0 else 1), second_to[half][way], i)

    for half in range(2):
        for way in range(2):
            send(piece(half, 0, 0), first_to[half][way], half * 4 + way)
    for half in range(2):
        send(piece(half, 0, 0), far_to[half], half * 4 + 2)
    for half in range(2):
        second(half, 0)
    share(panel.at[x, y, core], panel.at[x, y, 1 - core], 0)
    for half in range(2):
        arrive(piece(half, 3, 0), half * 4)
        arrive(piece(half, 1, 0), half * 4 + 1)
    for half in range(2):
        second(half, 3)
        second(half, 1)
    share(panel.at[xm, y, core, :, near], panel.at[xm, y, 1 - core, :, near], 1)
    share(panel.at[x, ym, core, :, far], panel.at[x, ym, 1 - core, :, far], 2)
    share(panel.at[xp, y, core, :, near], panel.at[xp, y, 1 - core, :, near], 3)
    share(panel.at[x, yp, core, :, far], panel.at[x, yp, 1 - core, :, far], 4)
    for half in range(2):
        second_arrive(half, 0, 0)
        second_pass(half, 0, 0)
    for half in range(2):
        arrive(piece(half, 2, 0), half * 4 + 2)
        second(half, 2)
    share(panel.at[xo, y, core, :, near], panel.at[xo, y, 1 - core, :, near], 5)
    share(panel.at[x, yo, core, :, far], panel.at[x, yo, 1 - core, :, far], 6)
    for half in range(2):
        second_arrive(half, 0, 1)
        second_arrive(half, 3, 1)
        second_pass(half, 3, 1)
        second_arrive(half, 1, 0)
        second_pass(half, 1, 0)

    row_hits = hits[:, 0:48]
    pextra[...] = 0.1 + 0.5 * spread(row_hits[0:32, 0:32], 32)
    extra[...] = 0.1 + 0.5 * spread(row_hits[32:40, 32:48], 16)

    for half in range(2):
        second_arrive(half, 3, 0)
        second_arrive(half, 1, 1)
    for half in range(2):
        second_arrive(half, 2, 1)
        second_pass(half, 2, 1)
        second_arrive(half, 2, 0)
    share(panel.at[:, ym, core, :, near], panel.at[:, ym, 1 - core, :, near], 7)
    share(panel.at[xm, :, core, :, far], panel.at[xm, :, 1 - core, :, far], 8)
    share(panel.at[:, yp, core, :, near], panel.at[:, yp, 1 - core, :, near], 9)
    share(panel.at[xp, :, core, :, far], panel.at[xp, :, 1 - core, :, far], 10)
    ring_arrive(1)
    ring_send(2)
    for half in range(2):
        for along in range(4):
            arrive(piece(half, along, 2), 16 + half * 12 + along)
    share(panel.at[:, yo, core, :, near], panel.at[:, yo, 1 - core, :, near], 11)
    share(panel.at[xo, :, core, :, far], panel.at[xo, :, 1 - core, :, far], 12)
    for c, back, i in passed:
        copy(back, twin, slot, cs.at[i], cr.at[i]).wait_recv()
        c.wait_send()
    visit_next().start()

    def panel_rows(n):
        return panel[n].reshape(256, 2048)

    def panel_squares(n, unused):
        for q in range(2):
            v = panel_rows(n)[q * LEAF : (q + 1) * LEAF, :].astype(F32)
            s = jnp.sum(v * v, axis=1, keepdims=True)
            at = slice(n * 256 + q * LEAF, n * 256 + (q + 1) * LEAF)
            psq_col[at, :] = jnp.broadcast_to(s, (LEAF, 128))
            psq_row[0:1, at] = to_lanes(s)
        return unused

    for n in range(SIDE):
        panel_squares(n, 0)

    def build(n, unused):
        cols = slice(n * 256, n * 256 + 256)
        g = dot_nt(panel[...].reshape(PANEL, 2048), panel_rows(n))
        s = psq_col[...]
        k = jnp.exp(-0.5 * (jnp.concatenate([s, s], axis=1) + psq_row[0:1, cols] - 2.0 * g))
        row = lax.broadcasted_iota(jnp.int32, (PANEL, 256), 0)
        lane = lax.broadcasted_iota(jnp.int32, (PANEL, 256), 1)
        a[:, cols] = k + jnp.where(row == lane + n * 256, pextra[0:1, cols], 0.0)
        return unused

    for n in range(SIDE):
        build(n, 0)

    def event(m):
        @pl.when(m == 1)
        def _():
            ring_arrive(2)
            ring_send(3)
            visit_arrive(0, 9)
            visit_relay().start()
            visit_straight().start()

        @pl.when(m == 4)
        def _():
            ring_arrive(3)
            ring_send(4)

        @pl.when(m == 5)
        def _():
            visit_arrive(1, 8 + 2 * core)
            visit_arrive(2, 10 - 2 * core)

        @pl.when(m == 6)
        def _():
            ring_arrive(4)

    lead_row = lax.broadcasted_iota(jnp.int32, (32, PANEL), 0)
    lead_lane = lax.broadcasted_iota(jnp.int32, (32, PANEL), 1)

    def kernel_rows(slices):
        parts = []
        for i, block_id, leads in slices:
            v = rows[i].astype(F32)
            parts.append(jnp.sum(v * v, axis=1, keepdims=True))
            sq_col[pl.ds(pl.multiple_of(i * LEAF, LEAF), LEAF), :] = jnp.broadcast_to(parts[-1], (LEAF, 128))
        left = jnp.concatenate([rows[i] for i, block_id, leads in slices], axis=0)
        g = dot_nt(left, panel[...].reshape(PANEL, 2048))
        k = jnp.exp(-0.5 * (jnp.concatenate(parts, axis=0) + psq_row[0:1, :] - 2.0 * g))
        for q, (i, block_id, leads) in enumerate(slices):
            hit = lead_lane == block_id * 32 + lead_row
            top_rows = k[q * LEAF : q * LEAF + 32, :] + jnp.where(hit, pextra[0:1, :] * leads, 0.0)
            high, lo = halves(jnp.concatenate([top_rows, k[q * LEAF + 32 : (q + 1) * LEAF, :]], axis=0))
            at = pl.ds(pl.multiple_of(i * LEAF, LEAF), LEAF)
            kh[at, :] = high
            kl[at, :] = lo

    def is_zero(i):
        return jnp.where(i == 0, 1.0, 0.0).astype(F32)

    def one_slice(m):
        away = (m + 1) // 2
        i = (slot + 8 + away - 2 * away * (m % 2)) % 8
        kernel_rows([(i, me, is_zero(i))])

    def two_slices(m):
        late, last = m // 5, m // 6
        early = 1 - late
        i = early * ((slot + 9 - m) % 8) + late * (4 + m)
        i_block = early * me + late * ((me + 35 - m) % 32)
        j = early * ((slot + m - 1) % 8) + (late - last) * 8 + last * ((slot + 4) % 8)
        j_block = (1 - late + last) * me + (late - last) * ((me + 31) % 32)
        i_slice = early * i + late * slot
        j_slice = (1 - late + last) * j + (late - last) * slot
        kernel_rows([(i, i_block, is_zero(i_slice)), (j, j_block, is_zero(j_slice))])

    chain_steps(a, leaf, low, up, xh, xl, event, one_slice, two_slices)
    own = pl.ds(pl.multiple_of(slot * LEAF, LEAF), LEAF)
    sq_row[0:1, 0:128] = sq_col[own, :].T[0:1, :]
    for s in range(3):
        sq_row[0:1, (s + 1) * LEAF : (s + 2) * LEAF] = sq_col[1024 + s * LEAF : 1024 + (s + 1) * LEAF, :].T[0:1, :]
    for n in range(4):
        depth = 256 * (n + 1)
        cols = slice(256 * n, 256 * n + 256)
        f = dot(kh[:, :depth], xh[:depth, cols])
        f = f + dot(kh[:, :depth], xl[:depth, cols])
        f = f + dot(kl[:, :depth], xh[:depth, cols])
        high, lo = halves(f)
        fh[:, cols] = high
        fl[:, cols] = lo
    factor_ref[...] = fh[own, :].astype(F32) + fl[own, :].astype(F32)
    vh[0:LEAF, :] = fh[own, :]
    vl[0:LEAF, :] = fl[own, :]
    vh[LEAF:, :] = fh[1024:, :]
    vl[LEAF:, :] = fl[1024:, :]
    r = lax.broadcasted_iota(jnp.int32, (1024, LEAF), 0)
    c = lax.broadcasted_iota(jnp.int32, (1024, LEAF), 1)

    def tile(h, unused):
        at = pl.ds(pl.multiple_of(h * 256, 256), 256)
        right = jnp.concatenate([rows[(1 - h) * slot + 9 * h], rows[8 + 2 * h]], axis=0)
        g = dot_nt(rows[0:8].reshape(1024, 2048), right)
        s = sq_col[0:1024, :]
        k = jnp.exp(-0.5 * (jnp.concatenate([s, s], axis=1) + sq_row[0:1, at] - 2.0 * g))
        ff = dot_nt(fh[0:1024, :], vh[at, :])
        ff = ff + dot_nt(fh[0:1024, :], vl[at, :])
        ff = ff + dot_nt(fl[0:1024, :], vh[at, :])
        t = k - ff
        diagonal = jnp.where(r == c + slot * LEAF, extra[0:1, :] * jnp.where(h == 0, 1.0, 0.0).astype(F32), 0.0)
        trail_ref[:, at] = jnp.concatenate([t[:, 0:LEAF] + diagonal, t[:, LEAF:]], axis=1)
        return unused

    lax.fori_loop(0, 2, tile, 0)
    for h in range(1, 5):
        ring_sent(h)
    visit_next().wait_send()
    visit_relay().wait_send()
    visit_straight().wait_send()
    for c in sent:
        c.wait_send()

    @pl.when(slot == 0)
    def _():
        for c in range(1, 8):
            copy(chunk(c), me, c, zs.at[c], zr.at[c]).wait_send()
            copy(chunk(0), me, c, zs.at[7 + c], zr.at[0]).wait_send()

    @pl.when(slot != 0)
    def _():
        for j in range(1, 8):
            other = (slot + j) % 8

            @pl.when(other != 0)
            def _(other=other, j=j):
                copy(chunk(slot), me, other, zs.at[j], zr.at[slot]).wait_send()


def whole(embeddings, inverse_scales, pairs):
    vmem = pl.BlockSpec(memory_space=pltpu.VMEM)
    total = 1024 + 3 * LEAF
    return pl.pallas_call(
        whole_kernel,
        out_shape=(
            jax.ShapeDtypeStruct((1024, STOPS * LEAF), F32),
            jax.ShapeDtypeStruct((LEAF, PANEL), F32),
        ),
        in_specs=[vmem] * 3,
        out_specs=(vmem, vmem),
        scratch_shapes=[
            pltpu.VMEM((11, LEAF, 2048), BF16),
            pltpu.VMEM((SIDE, SIDE, 2, 32, 2048), BF16),
            pltpu.VMEM((1, PANEL), F32),
            pltpu.VMEM((1, LEAF), F32),
            pltpu.VMEM((48, 128), F32),
            pltpu.VMEM((PANEL, PANEL), F32),
            pltpu.VMEM((LEAF, LEAF), F32),
            pltpu.VMEM((PANEL, 3 * LEAF), BF16),
            pltpu.VMEM((3 * LEAF, PANEL), BF16),
            pltpu.VMEM((PANEL, 128), F32),
            pltpu.VMEM((1, PANEL), F32),
            pltpu.VMEM((total, 128), F32),
            pltpu.VMEM((1, STOPS * LEAF), F32),
            pltpu.VMEM((total, PANEL), BF16),
            pltpu.VMEM((total, PANEL), BF16),
            pltpu.VMEM((PANEL, PANEL), BF16),
            pltpu.VMEM((PANEL, PANEL), BF16),
            pltpu.VMEM((total, PANEL), BF16),
            pltpu.VMEM((total, PANEL), BF16),
            pltpu.VMEM((STOPS * LEAF, PANEL), BF16),
            pltpu.VMEM((STOPS * LEAF, PANEL), BF16),
            pltpu.SemaphoreType.DMA((15,)),
            pltpu.SemaphoreType.DMA((8,)),
            pltpu.SemaphoreType.DMA((32,)),
            pltpu.SemaphoreType.DMA((32,)),
            pltpu.SemaphoreType.DMA((13,)),
            pltpu.SemaphoreType.DMA((13,)),
            pltpu.SemaphoreType.DMA((8,)),
            pltpu.SemaphoreType.DMA((8,)),
            pltpu.SemaphoreType.DMA((3,)),
            pltpu.SemaphoreType.DMA((3,)),
        ],
        compiler_params=pltpu.CompilerParams(
            collective_id=0, has_side_effects=True, vmem_limit_bytes=44 << 20
        ),
        name="whole",
    )(embeddings, inverse_scales, pairs)


def body(embeddings, inverse_scales, matches):
    pairs = matches.reshape(-1, 128, 2).transpose(0, 2, 1).reshape(-1, 128)
    return whole(embeddings, inverse_scales[None, :], pairs)


def solution(mesh):
    return jax.shard_map(
        body,
        mesh=mesh,
        in_specs=(P(("row", "col"), None), P(), P()),
        out_specs=(P("row", "col"), P(("row", "col"), None)),
        check_vma=False,
    )
```

```python
import functools

import jax
import jax.numpy as jnp
from jax import lax
from jax.experimental import pallas as pl
from jax.experimental.pallas import tpu as pltpu
from jax.sharding import PartitionSpec as P

PANEL = 1024
STOPS = 4
LEAF = 128
AHEAD = 4
F32 = jnp.float32
BF16 = jnp.bfloat16


def halves(x):
    high = x.astype(BF16)
    return high, (x - high.astype(F32)).astype(BF16)


def dot(a, b):
    return jnp.dot(a, b, preferred_element_type=F32)


def dot_nt(a, b):
    return lax.dot_general(a, b, (((1,), (1,)), ((), ())), preferred_element_type=F32)


def leaf_factor(tile, out_ref):
    n = LEAF
    groups = n // 8
    lane = lax.broadcasted_iota(jnp.int32, (8, 128), 1)
    rows = [tile[8 * i : 8 * i + 8, :] for i in range(groups)]

    def column(i, k):
        return jnp.broadcast_to(rows[i][:, k : k + 1], (8, 128))

    def one_row(x, r):
        return jnp.broadcast_to(x[r : r + 1, :], (8, 128))

    pending = [[column(i, k) for i in range(groups)] for k in range(AHEAD)]
    for k in range(n):
        g, r = divmod(k, 8)
        current = pending.pop(0)
        scale = lax.rsqrt(one_row(current[g], r))
        c = [current[i] * scale if i >= g else None for i in range(groups)]
        if k + AHEAD < n:
            pending.append([column(i, k + AHEAD) if i >= (k + AHEAD) // 8 else None for i in range(groups)])
        for j in range(len(pending)):
            gp, rp = divmod(k + 1 + j, 8)
            s = one_row(c[gp], rp)
            pending[j] = [pending[j][i] - c[i] * s if i >= gp else None for i in range(groups)]
        u = jnp.where(lane == k, scale, one_row(rows[g], r) * scale)
        out_ref[k : k + 1, :] = u[0:1, :]
        for i in range(g, groups):
            rows[i] = jnp.where(lane == k, 0.0, rows[i]) - c[i] * u


MESH = pl.DeviceIdType.MESH
SIDE = 4


def counts_step(values, first):
    sub32 = lax.broadcasted_iota(jnp.int32, (32, 128), 0)
    sub16 = lax.broadcasted_iota(jnp.int32, (16, 128), 0)
    block = values >> 10
    place = jnp.where((values & 1023) < 32, values & 31, -1)
    inside = values - first
    part = jnp.where((inside >= 0) & (inside < 128), inside >> 4, -1)
    unit = values & 15

    def marks(big, small, r):
        return jnp.concatenate(
            [
                jnp.where(sub32 == big[r : r + 1, :], 1.0, 0.0).astype(BF16),
                jnp.where(sub16 == small[r : r + 1, :], 1.0, 0.0).astype(BF16),
            ],
            axis=0,
        )

    return [marks(block, part, r) for r in range(8)], [marks(place, unit, r) for r in range(8)]


def spread(table, width):
    n = table.shape[0]
    total = n * width
    tiled = jnp.concatenate([table] * n, axis=1)
    row = lax.broadcasted_iota(jnp.int32, (n, total), 0)
    lane = lax.broadcasted_iota(jnp.int32, (n, total), 1)
    return jnp.sum(jnp.where(lane >> (width.bit_length() - 1) == row, tiled, 0.0), axis=0, keepdims=True)


def to_lanes(column):
    return jnp.broadcast_to(column, (128, 128)).T[0:1, :]


def chain_steps(a, leaf, low, up, xh, xl, event, one_slice, two_slices):
    count = PANEL // LEAF
    r128 = lax.broadcasted_iota(jnp.int32, (LEAF, LEAF), 0)
    c128 = lax.broadcasted_iota(jnp.int32, (LEAF, LEAF), 1)
    lane = lax.broadcasted_iota(jnp.int32, (LEAF, PANEL), 1)

    def beside(x):
        high, lo = halves(x)
        return jnp.concatenate([high, high, lo], axis=1)

    def above(x):
        high, lo = halves(x)
        return jnp.concatenate([high, lo, high], axis=0)

    def inverse():
        w = jnp.where(r128 >= c128, leaf[...], 0.0)
        return w, w.T

    def block(k):
        return pl.ds(pl.multiple_of(k * LEAF, LEAF), LEAF)

    def finish_column(m, lcol, wt):
        low[...] = beside(lcol)
        low[block(m), :] = beside(wt)
        row = lax.broadcasted_iota(jnp.int32, (PANEL, LEAF), 0)
        for half, out in ((slice(0, LEAF), xh), (slice(2 * LEAF, 3 * LEAF), xl)):
            out[:, block(m)] = jnp.where(row < (m + 1) * LEAF, low[:, half].astype(F32), 0.0).astype(BF16)

    leaf_factor(a[0:LEAF, 0:LEAF], leaf)

    def step(beside_leaf, m, unused):
        event(m)
        own, after = block(m), block(m + 1)
        w, wt = inverse()
        w3, t3 = beside(w), above(wt)
        next_low = dot(beside(a[after, own]), t3)
        next_up = dot(w3, above(a[own, after]))
        tile = a[after, after] - dot(beside(next_low), above(next_up))
        finish_column(m, dot(beside(a[:, own]), t3), wt)
        mine = a[own, :]
        later = lane >= (m + 1) * LEAF
        up[...] = above(jnp.where(later, dot(w3, above(mine)), 0.0))
        a[own, :] = jnp.where(later, 0.0, mine)
        for n in range(PANEL // 256):
            cols = slice(256 * n, 256 * n + 256)
            a[:, cols] = a[:, cols] - dot(low[...], up[:, cols])
        beside_leaf(m)
        leaf_factor(tile, leaf)
        return unused

    lax.fori_loop(0, 3, functools.partial(step, one_slice), 0)
    lax.fori_loop(3, count - 1, functools.partial(step, two_slices), 0)
    last = block(count - 1)
    w, wt = inverse()
    finish_column(count - 1, dot(beside(a[:, last]), above(wt)), wt)


def whole_kernel(
    emb_ref, inv_ref, pairs_ref, trail_ref, factor_ref,
    rows, panel, pextra, extra, hits, a, leaf, low, up, psq_col, psq_row, sq_col, sq_row,
    kh, kl, xh, xl, fh, fl, vh, vl, zs, zr, ss, sr, cs, cr, bs, br, vs, vr,
):
    me = lax.axis_index("row")
    slot = lax.axis_index("col")
    x, y, core = me // 8, (me // 2) % SIDE, me % 2
    xp, xm, xo = (x + 1) % SIDE, (x + 3) % SIDE, (x + 2) % SIDE
    yp, ym, yo = (y + 1) % SIDE, (y + 3) % SIDE, (y + 2) % SIDE

    def row_at(x, y, core):
        return (x * SIDE + y) * 2 + core

    to_xp, to_xm = row_at(xp, y, core), row_at(xm, y, core)
    to_yp, to_ym = row_at(x, yp, core), row_at(x, ym, core)
    twin = row_at(x, y, 1 - core)
    barrier = pltpu.get_barrier_semaphore()
    for other in (to_xp, to_xm, to_yp, to_ym, twin, row_at(xo, y, core), row_at(x, yo, core)):
        pl.semaphore_signal(barrier, inc=1, device_id=(other, slot), device_id_type=MESH)
    for j in range(1, 8):
        pl.semaphore_signal(barrier, inc=1, device_id=(me, (slot + j) % 8), device_id_type=MESH)
    for j in range(1, STOPS):
        pl.semaphore_signal(barrier, inc=1, device_id=((me + j) % 32, slot), device_id_type=MESH)
        pl.semaphore_signal(barrier, inc=1, device_id=((me + 32 - j) % 32, slot), device_id_type=MESH)

    def scale(start, count):
        v = emb_ref[start : start + count, :].astype(F32) * inv_ref[0:1, :]
        rows[slot, start : start + count, :] = v.astype(BF16)

    scale(0, 32)

    @pl.when(slot == 0)
    def _():
        panel[x, y, core] = rows[slot, 0:32, :]

    pl.semaphore_wait(barrier, 14 + 2 * (STOPS - 1))

    def copy(view, row, col, send, recv):
        return pltpu.make_async_remote_copy(
            src_ref=view, dst_ref=view, send_sem=send, recv_sem=recv, device_id=(row, col), device_id_type=MESH
        )

    def chunk(q):
        return panel.at[x, y, core, :, pl.ds(pl.multiple_of(q * 256, 256), 256)]

    @pl.when(slot == 0)
    def _():
        for c in range(1, 8):
            copy(chunk(c), me, c, zs.at[c], zr.at[c]).start()
        for c in range(1, 8):
            copy(chunk(0), me, c, zs.at[7 + c], zr.at[0]).start()

    scale(32, 96)

    @pl.when(slot != 0)
    def _():
        copy(chunk(slot), me, slot, zs.at[0], zr.at[slot]).wait_recv()
        for j in range(1, 8):
            other = (slot + j) % 8

            @pl.when(other != 0)
            def _(other=other, j=j):
                copy(chunk(slot), me, other, zs.at[j], zr.at[slot]).start()

    first = row_at(x, y, core) * 1024 + slot * 128

    def count(i, total):
        lefts, rights = [], []
        for q in range(4):
            left, right = counts_step(pairs_ref[pl.ds(pl.multiple_of(i * 32 + q * 8, 8), 8), :], first)
            lefts += left
            rights += right
        return total + dot_nt(jnp.concatenate(lefts, axis=1), jnp.concatenate(rights, axis=1))

    hits[:, 0:48] = lax.fori_loop(0, pairs_ref.shape[0] // 32, count, jnp.zeros((48, 48), F32))

    @pl.when(slot != 0)
    def _():
        for j in range(1, 8):
            other = (slot + j) % 8
            copy(chunk(other), me, slot, zs.at[0], zr.at[other]).wait_recv()

    upper, lower = pl.ds(0, 64), pl.ds(64, 64)

    def ring_views(h):
        up, down = (slot + 9 - h) % 8, (slot + 7 + h) % 8
        if h < 4:
            return rows.at[up], rows.at[down]
        return rows.at[up, upper], rows.at[down, lower]

    def arriving_views(h):
        up, down = (slot + 8 - h) % 8, (slot + h) % 8
        if h < 4:
            return rows.at[up], rows.at[down]
        return rows.at[up, upper], rows.at[down, lower]

    def ring_send(h):
        up, down = ring_views(h)
        copy(up, me, (slot + 1) % 8, bs.at[2 * h - 2], br.at[2 * h - 2]).start()
        copy(down, me, (slot + 7) % 8, bs.at[2 * h - 1], br.at[2 * h - 1]).start()

    def ring_arrive(h):
        up, down = arriving_views(h)
        copy(up, me, slot, bs.at[2 * h - 2], br.at[2 * h - 2]).wait_recv()
        copy(down, me, slot, bs.at[2 * h - 1], br.at[2 * h - 1]).wait_recv()

    def ring_sent(h):
        up, down = ring_views(h)
        copy(up, me, slot, bs.at[2 * h - 2], br.at[2 * h - 2]).wait_send()
        copy(down, me, slot, bs.at[2 * h - 1], br.at[2 * h - 1]).wait_send()

    def visitor_copy(src, dst, row, i):
        return pltpu.make_async_remote_copy(
            src_ref=rows.at[src], dst_ref=rows.at[dst], send_sem=vs.at[i], recv_sem=vr.at[i],
            device_id=(row, slot), device_id_type=MESH,
        )

    def visit_next():
        return visitor_copy(slot, 9, (me + 2) % 32, 0)

    def visit_relay():
        return visitor_copy(9, 10 - 2 * core, twin, 1)

    def visit_straight():
        return visitor_copy(slot, 8 + 2 * core, (me + 1 + 2 * core) % 32, 2)

    def visit_arrive(i, at):
        visitor_copy(at, at, twin, i).wait_recv()

    ring_send(1)
    near, far = pl.ds(0, 1024), pl.ds(1024, 1024)
    sent = []

    def send(view, row, i):
        c = copy(view, row, slot, ss.at[i], sr.at[i])
        c.start()
        sent.append(c)

    def arrive(view, i):
        copy(view, twin, slot, ss.at[i], sr.at[i]).wait_recv()

    passed = []

    def share(view, back, i):
        c = copy(view, twin, slot, cs.at[i], cr.at[i])
        c.start()
        passed.append((c, back, i))

    xs, ys = (x, xp, xo, xm), (y, yp, yo, ym)

    def piece(half, along, across, which=core):
        if half == 0:
            return panel.at[xs[along], ys[across], which, :, near]
        return panel.at[xs[across], ys[along], which, :, far]

    first_to = ((to_xp, to_xm), (to_yp, to_ym))
    far_to = (row_at(xo, y, core), row_at(x, yo, core))
    second_to = ((to_yp, to_ym), (to_xp, to_xm))

    def second(half, along):
        for way in range(2):
            send(piece(half, along, 0), second_to[half][way], 8 + half * 12 + along * 2 + way)

    def second_arrive(half, along, way):
        arrive(piece(half, along, 3 if way == 0 else 1), 8 + half * 12 + along * 2 + way)

    def second_pass(half, along, way):
        i = 16 + half * 12 + along
        send(piece(half, along, 3 if way == 0 else 1), second_to[half][way], i)

    for half in range(2):
        for way in range(2):
            send(piece(half, 0, 0), first_to[half][way], half * 4 + way)
    for half in range(2):
        send(piece(half, 0, 0), far_to[half], half * 4 + 2)
    for half in range(2):
        second(half, 0)
    share(panel.at[x, y, core], panel.at[x, y, 1 - core], 0)
    for half in range(2):
        arrive(piece(half, 3, 0), half * 4)
        arrive(piece(half, 1, 0), half * 4 + 1)
    for half in range(2):
        second(half, 3)
        second(half, 1)
    share(panel.at[xm, y, core, :, near], panel.at[xm, y, 1 - core, :, near], 1)
    share(panel.at[x, ym, core, :, far], panel.at[x, ym, 1 - core, :, far], 2)
    share(panel.at[xp, y, core, :, near], panel.at[xp, y, 1 - core, :, near], 3)
    share(panel.at[x, yp, core, :, far], panel.at[x, yp, 1 - core, :, far], 4)
    for half in range(2):
        second_arrive(half, 0, 0)
        second_pass(half, 0, 0)
    for half in range(2):
        arrive(piece(half, 2, 0), half * 4 + 2)
        second(half, 2)
    share(panel.at[xo, y, core, :, near], panel.at[xo, y, 1 - core, :, near], 5)
    share(panel.at[x, yo, core, :, far], panel.at[x, yo, 1 - core, :, far], 6)
    for half in range(2):
        second_arrive(half, 0, 1)
        second_arrive(half, 3, 1)
        second_pass(half, 3, 1)
        second_arrive(half, 1, 0)
        second_pass(half, 1, 0)

    row_hits = hits[:, 0:48]
    pextra[...] = 0.1 + 0.5 * spread(row_hits[0:32, 0:32], 32)
    extra[...] = 0.1 + 0.5 * spread(row_hits[32:40, 32:48], 16)

    for half in range(2):
        second_arrive(half, 3, 0)
        second_arrive(half, 1, 1)
    for half in range(2):
        second_arrive(half, 2, 1)
        second_pass(half, 2, 1)
        second_arrive(half, 2, 0)
    share(panel.at[:, ym, core, :, near], panel.at[:, ym, 1 - core, :, near], 7)
    share(panel.at[xm, :, core, :, far], panel.at[xm, :, 1 - core, :, far], 8)
    share(panel.at[:, yp, core, :, near], panel.at[:, yp, 1 - core, :, near], 9)
    share(panel.at[xp, :, core, :, far], panel.at[xp, :, 1 - core, :, far], 10)
    ring_arrive(1)
    ring_send(2)
    for along in (0, 3, 1, 2):
        for half in range(2):
            arrive(piece(half, along, 2), 16 + half * 12 + along)
            share(piece(half, along, 2), piece(half, along, 2, 1 - core), 11 + half * 4 + along)
    for c, back, i in passed:
        copy(back, twin, slot, cs.at[i], cr.at[i]).wait_recv()
        c.wait_send()
    visit_next().start()

    def panel_rows(n):
        return panel[n].reshape(256, 2048)

    def panel_squares(n, unused):
        for q in range(2):
            v = panel_rows(n)[q * LEAF : (q + 1) * LEAF, :].astype(F32)
            s = jnp.sum(v * v, axis=1, keepdims=True)
            at = slice(n * 256 + q * LEAF, n * 256 + (q + 1) * LEAF)
            psq_col[at, :] = jnp.broadcast_to(s, (LEAF, 128))
            psq_row[0:1, at] = to_lanes(s)
        return unused

    for n in range(SIDE):
        panel_squares(n, 0)

    def build(n, unused):
        cols = slice(n * 256, n * 256 + 256)
        g = dot_nt(panel[...].reshape(PANEL, 2048), panel_rows(n))
        s = psq_col[...]
        k = jnp.exp(-0.5 * (jnp.concatenate([s, s], axis=1) + psq_row[0:1, cols] - 2.0 * g))
        row = lax.broadcasted_iota(jnp.int32, (PANEL, 256), 0)
        lane = lax.broadcasted_iota(jnp.int32, (PANEL, 256), 1)
        a[:, cols] = k + jnp.where(row == lane + n * 256, pextra[0:1, cols], 0.0)
        return unused

    for n in range(SIDE):
        build(n, 0)

    def event(m):
        @pl.when(m == 1)
        def _():
            ring_arrive(2)
            ring_send(3)
            visit_arrive(0, 9)
            visit_relay().start()
            visit_straight().start()

        @pl.when(m == 4)
        def _():
            ring_arrive(3)
            ring_send(4)

        @pl.when(m == 5)
        def _():
            visit_arrive(1, 8 + 2 * core)
            visit_arrive(2, 10 - 2 * core)

        @pl.when(m == 6)
        def _():
            ring_arrive(4)

    lead_row = lax.broadcasted_iota(jnp.int32, (32, PANEL), 0)
    lead_lane = lax.broadcasted_iota(jnp.int32, (32, PANEL), 1)

    def kernel_rows(slices):
        parts = []
        for i, block_id, leads in slices:
            v = rows[i].astype(F32)
            parts.append(jnp.sum(v * v, axis=1, keepdims=True))
            sq_col[pl.ds(pl.multiple_of(i * LEAF, LEAF), LEAF), :] = jnp.broadcast_to(parts[-1], (LEAF, 128))
        left = jnp.concatenate([rows[i] for i, block_id, leads in slices], axis=0)
        g = dot_nt(left, panel[...].reshape(PANEL, 2048))
        k = jnp.exp(-0.5 * (jnp.concatenate(parts, axis=0) + psq_row[0:1, :] - 2.0 * g))
        for q, (i, block_id, leads) in enumerate(slices):
            hit = lead_lane == block_id * 32 + lead_row
            top_rows = k[q * LEAF : q * LEAF + 32, :] + jnp.where(hit, pextra[0:1, :] * leads, 0.0)
            high, lo = halves(jnp.concatenate([top_rows, k[q * LEAF + 32 : (q + 1) * LEAF, :]], axis=0))
            at = pl.ds(pl.multiple_of(i * LEAF, LEAF), LEAF)
            kh[at, :] = high
            kl[at, :] = lo

    def is_zero(i):
        return jnp.where(i == 0, 1.0, 0.0).astype(F32)

    def one_slice(m):
        away = (m + 1) // 2
        i = (slot + 8 + away - 2 * away * (m % 2)) % 8
        kernel_rows([(i, me, is_zero(i))])

    def two_slices(m):
        late, last = m // 5, m // 6
        early = 1 - late
        i = early * ((slot + 9 - m) % 8) + late * (4 + m)
        i_block = early * me + late * ((me + 35 - m) % 32)
        j = early * ((slot + m - 1) % 8) + (late - last) * 8 + last * ((slot + 4) % 8)
        j_block = (1 - late + last) * me + (late - last) * ((me + 31) % 32)
        i_slice = early * i + late * slot
        j_slice = (1 - late + last) * j + (late - last) * slot
        kernel_rows([(i, i_block, is_zero(i_slice)), (j, j_block, is_zero(j_slice))])

    chain_steps(a, leaf, low, up, xh, xl, event, one_slice, two_slices)
    own = pl.ds(pl.multiple_of(slot * LEAF, LEAF), LEAF)
    sq_row[0:1, 0:128] = sq_col[own, :].T[0:1, :]
    for s in range(3):
        sq_row[0:1, (s + 1) * LEAF : (s + 2) * LEAF] = sq_col[1024 + s * LEAF : 1024 + (s + 1) * LEAF, :].T[0:1, :]
    for n in range(4):
        depth = 256 * (n + 1)
        cols = slice(256 * n, 256 * n + 256)
        f = dot(kh[:, :depth], xh[:depth, cols])
        f = f + dot(kh[:, :depth], xl[:depth, cols])
        f = f + dot(kl[:, :depth], xh[:depth, cols])
        high, lo = halves(f)
        fh[:, cols] = high
        fl[:, cols] = lo
    factor_ref[...] = fh[own, :].astype(F32) + fl[own, :].astype(F32)
    vh[0:LEAF, :] = fh[own, :]
    vl[0:LEAF, :] = fl[own, :]
    vh[LEAF:, :] = fh[1024:, :]
    vl[LEAF:, :] = fl[1024:, :]
    r = lax.broadcasted_iota(jnp.int32, (1024, LEAF), 0)
    c = lax.broadcasted_iota(jnp.int32, (1024, LEAF), 1)

    def tile(h, unused):
        at = pl.ds(pl.multiple_of(h * 256, 256), 256)
        right = jnp.concatenate([rows[(1 - h) * slot + 9 * h], rows[8 + 2 * h]], axis=0)
        g = dot_nt(rows[0:8].reshape(1024, 2048), right)
        s = sq_col[0:1024, :]
        k = jnp.exp(-0.5 * (jnp.concatenate([s, s], axis=1) + sq_row[0:1, at] - 2.0 * g))
        ff = dot_nt(fh[0:1024, :], vh[at, :])
        ff = ff + dot_nt(fh[0:1024, :], vl[at, :])
        ff = ff + dot_nt(fl[0:1024, :], vh[at, :])
        t = k - ff
        diagonal = jnp.where(r == c + slot * LEAF, extra[0:1, :] * jnp.where(h == 0, 1.0, 0.0).astype(F32), 0.0)
        trail_ref[:, at] = jnp.concatenate([t[:, 0:LEAF] + diagonal, t[:, LEAF:]], axis=1)
        return unused

    lax.fori_loop(0, 2, tile, 0)
    for h in range(1, 5):
        ring_sent(h)
    visit_next().wait_send()
    visit_relay().wait_send()
    visit_straight().wait_send()
    for c in sent:
        c.wait_send()

    @pl.when(slot == 0)
    def _():
        for c in range(1, 8):
            copy(chunk(c), me, c, zs.at[c], zr.at[c]).wait_send()
            copy(chunk(0), me, c, zs.at[7 + c], zr.at[0]).wait_send()

    @pl.when(slot != 0)
    def _():
        for j in range(1, 8):
            other = (slot + j) % 8

            @pl.when(other != 0)
            def _(other=other, j=j):
                copy(chunk(slot), me, other, zs.at[j], zr.at[slot]).wait_send()


def whole(embeddings, inverse_scales, pairs):
    vmem = pl.BlockSpec(memory_space=pltpu.VMEM)
    total = 1024 + 3 * LEAF
    return pl.pallas_call(
        whole_kernel,
        out_shape=(
            jax.ShapeDtypeStruct((1024, STOPS * LEAF), F32),
            jax.ShapeDtypeStruct((LEAF, PANEL), F32),
        ),
        in_specs=[vmem] * 3,
        out_specs=(vmem, vmem),
        scratch_shapes=[
            pltpu.VMEM((11, LEAF, 2048), BF16),
            pltpu.VMEM((SIDE, SIDE, 2, 32, 2048), BF16),
            pltpu.VMEM((1, PANEL), F32),
            pltpu.VMEM((1, LEAF), F32),
            pltpu.VMEM((48, 128), F32),
            pltpu.VMEM((PANEL, PANEL), F32),
            pltpu.VMEM((LEAF, LEAF), F32),
            pltpu.VMEM((PANEL, 3 * LEAF), BF16),
            pltpu.VMEM((3 * LEAF, PANEL), BF16),
            pltpu.VMEM((PANEL, 128), F32),
            pltpu.VMEM((1, PANEL), F32),
            pltpu.VMEM((total, 128), F32),
            pltpu.VMEM((1, STOPS * LEAF), F32),
            pltpu.VMEM((total, PANEL), BF16),
            pltpu.VMEM((total, PANEL), BF16),
            pltpu.VMEM((PANEL, PANEL), BF16),
            pltpu.VMEM((PANEL, PANEL), BF16),
            pltpu.VMEM((total, PANEL), BF16),
            pltpu.VMEM((total, PANEL), BF16),
            pltpu.VMEM((STOPS * LEAF, PANEL), BF16),
            pltpu.VMEM((STOPS * LEAF, PANEL), BF16),
            pltpu.SemaphoreType.DMA((15,)),
            pltpu.SemaphoreType.DMA((8,)),
            pltpu.SemaphoreType.DMA((32,)),
            pltpu.SemaphoreType.DMA((32,)),
            pltpu.SemaphoreType.DMA((19,)),
            pltpu.SemaphoreType.DMA((19,)),
            pltpu.SemaphoreType.DMA((8,)),
            pltpu.SemaphoreType.DMA((8,)),
            pltpu.SemaphoreType.DMA((3,)),
            pltpu.SemaphoreType.DMA((3,)),
        ],
        compiler_params=pltpu.CompilerParams(
            collective_id=0, has_side_effects=True, vmem_limit_bytes=44 << 20
        ),
        name="whole",
    )(embeddings, inverse_scales, pairs)


def body(embeddings, inverse_scales, matches):
    pairs = matches.reshape(-1, 128, 2).transpose(0, 2, 1).reshape(-1, 128)
    return whole(embeddings, inverse_scales[None, :], pairs)


def solution(mesh):
    return jax.shard_map(
        body,
        mesh=mesh,
        in_specs=(P(("row", "col"), None), P(), P()),
        out_specs=(P("row", "col"), P(("row", "col"), None)),
        check_vma=False,
    )
```
